256 devices in a mesh: node: 4 (over x), row: 16 (over z, core), col: 4 (over y).
Axes of the slice: x: 4, y: 4, z: 8, core: 2. Of those that a mesh axis runs over, the one named last changes fastest.
Arguments:
- basis_u: float32 [3, 64, 131072], P(None, 'col', ('node', 'row')), may hold values from -0.6 to 0.6
- basis_v: float32 [3, 64, 131072], P(None, 'col', ('node', 'row')), may hold values from -0.025 to 0.025
- leaf_diag: float32 [131072], P(('node', 'row')), may hold values from 1 to 4
- right_side: bfloat16 [1536, 131072], P('col', ('node', 'row')), may hold values from -6 to 6
- leaf_len: int32 [64], P(('node', 'row')), may hold values from 1 to 2048, 81920 in all
- ranks: int32 [3], replicated, may hold values from 32 to 64, as said below
Outputs:
- solution: float32 [1536, 131072], P('col', ('node', 'row'))
The draws below stay inside these ranges and needn't reach their ends.
Inputs may be any that keep to these rules, and one draw needn't show every extreme that they name: `leaf_len`: some row block has all 2048 rows live. `ranks`: one level has rank 64.
All inputs are finite; a program needn't handle non-finite values.
Results may differ from the reference program's by a relative error of at most 0.0003.
Values sent between devices are 32-bit elements; how exact they have to be, the bound alone decides.
A program may use at most 64 MiB of HBM per device.

```python
import math
import jax
import jax.numpy as jnp
import numpy as np
from jax import lax

RANK = 64
ROW_DEV = 2048
LEVELS = 3
GROUPS = 64
NTOT = 131072
NRHS = 1536
LIVE_ROWS = 81920


def draw_ranks(key, part):
    key = jax.random.fold_in(key, 7)
    first, second = jax.random.split(key)
    values = jax.random.randint(first, (LEVELS,), RANK // 2, RANK + 1)
    which = jax.random.randint(second, (), 0, LEVELS)
    return jnp.where(jnp.arange(LEVELS) == which, RANK, values).astype(jnp.int32)


def draw_basis_u(key, part):
    key = jax.random.fold_in(key, 11)
    shape = (LEVELS, RANK, NTOT)
    base = jnp.clip(jax.random.normal(key, shape, jnp.float32), -6.0, 6.0)
    return (0.1 * base).astype(jnp.float32)


def draw_basis_v(key, part):
    key = jax.random.fold_in(key, 13)
    shape = (LEVELS, RANK, NTOT)
    base = jnp.clip(jax.random.normal(key, shape, jnp.float32), -4.0, 4.0)
    levels = jnp.arange(LEVELS).astype(jnp.float32)
    block_rows = NTOT * jnp.exp2(levels) / 8.0
    spread = 0.8 / jnp.sqrt(block_rows)
    return (base * spread[:, None, None]).astype(jnp.float32)


def steps_of(rng, dims, cuts, smallest, largest):
    def one(dim, parts):
        draws = jax.random.uniform(jax.random.fold_in(jax.random.fold_in(rng, 6), dim), (parts,), jnp.float32, smallest / len(cuts), largest / len(cuts))
        return jnp.repeat(jnp.exp(draws), dims[dim] // parts).reshape((-1,) + (1,) * (len(dims) - dim - 1))

    factor_of = one(*cuts[0])
    for cut in cuts[1:]:
        factor_of = factor_of * one(*cut)
    return factor_of


def profile(number_of, total, reach, lean):
    weights = [(1 << 20) // math.isqrt(rank ** lean) + 1 for rank in range(2, number_of + 1)]
    rest, given = total - reach - (number_of - 1), [1] * (number_of - 1)
    while rest > 0:
        candidates = [i for i in range(number_of - 1) if given[i] < reach]
        mass, remaining = sum([weights[i] for i in candidates]), rest
        for i in candidates:
            more = min(reach - given[i], max(1, remaining * weights[i] // mass), rest)
            given[i] = given[i] + more
            rest = rest - more
    return np.array([reach] + given)


def uneven(rng, count, total, reach, skew):
    if count == 2:
        one = jax.random.randint(rng, (), max(1, total - reach), min(reach, total - 1) + 1)
        return jnp.stack([one, total - one])
    lengths = jnp.asarray(profile(count, total, reach, skew), jnp.int32)
    twos = (count - 1) // 2
    donor, receiver = lengths[1:1 + 2 * twos:2], lengths[2:2 + 2 * twos:2]
    slack = jnp.minimum(donor - 1, reach - receiver)
    moved = jax.random.randint(jax.random.fold_in(rng, 1), (twos,), 0, 1 << 20) % (slack + 1)
    lengths = lengths.at[1:1 + 2 * twos:2].set(donor - moved).at[2:2 + 2 * twos:2].set(receiver + moved)
    return lengths[jax.random.permutation(jax.random.fold_in(rng, 2), count)]


def normal_values(stream_key, shape, deviation, bound, cuts=(), held_as=jnp.bfloat16):
    values = deviation * jax.random.normal(stream_key, shape, jnp.float32)
    if cuts:
        values = values * steps_of(stream_key, shape, cuts, -0.22, 0.18)
    return jnp.clip(values, -bound, bound).astype(held_as)


def setup_inputs(seed: int = 0) -> dict:
    arg_keys = jax.random.split(jax.random.key(seed), 7)
    return {
        "basis_u": draw_basis_u(jax.random.fold_in(arg_keys[6], 71), 0),
        "basis_v": draw_basis_v(jax.random.fold_in(arg_keys[6], 71), 0),
        "leaf_diag": jnp.clip(jnp.exp(math.log(4.0) - 1.3862944 * jax.random.uniform(arg_keys[2], (NTOT,), jnp.float32) ** steps_of(arg_keys[2], (NTOT,), ((0, 64),), -0.2, 0.2)), 1.0, 4.0),
        "right_side": normal_values(arg_keys[3], (NRHS, NTOT), 1.0, 6.0, ((0, 4), (1, 64))),
        "leaf_len": uneven(arg_keys[4], GROUPS, LIVE_ROWS, ROW_DEV, 2).astype(jnp.int32),
        "ranks": draw_ranks(jax.random.fold_in(arg_keys[6], 71), 0),
    }


def eliminate(matrix, rhs):
    size = matrix.shape[0]
    augmented = jnp.concatenate([matrix, rhs], axis=1)

    def step(index, augmented):
        pivot_row = lax.dynamic_slice_in_dim(augmented, index, 1, 0)
        pivot = lax.dynamic_slice_in_dim(pivot_row, index, 1, 1)
        pivot_row = pivot_row / pivot
        column = lax.dynamic_slice_in_dim(augmented, index, 1, 1)
        hit = jnp.arange(size)[:, None] == index
        return jnp.where(hit, pivot_row, augmented - column * pivot_row)

    augmented = lax.fori_loop(0, size, step, augmented)
    return augmented[:, size:]


def reference(basis_u, basis_v, leaf_diag, right_side, leaf_len, ranks):
    high = lax.Precision.HIGHEST
    live = (jnp.arange(ROW_DEV)[None, :] < leaf_len[:, None]).astype(jnp.float32).reshape(NTOT)
    keep = (jnp.arange(RANK)[None, :] < ranks[:, None]).astype(jnp.float32)
    u_live = basis_u * live[None, None, :] * keep[:, :, None]
    v_live = basis_v * live[None, None, :] * keep[:, :, None]
    stack = jnp.concatenate([u_live[0], u_live[1], u_live[2], right_side.astype(jnp.float32)], 0)
    stack = stack / leaf_diag[None, :]
    eye = jnp.eye(RANK, dtype=jnp.float32)
    for level in range(LEVELS):
        blocks = 8 >> level
        width = NTOT // blocks
        count = stack.shape[0]
        v_blocks = v_live[level].reshape(RANK, blocks, width)
        s_blocks = stack.reshape(count, blocks, width)
        proj = jnp.einsum("ibr,jbr->bij", v_blocks, s_blocks, precision=high)
        sibling = proj[jnp.array([b ^ 1 for b in range(blocks)])]
        g_own = proj[:, :, :RANK]
        g_sib = sibling[:, :, :RANK]
        q_own = proj[:, :, RANK:]
        q_sib = sibling[:, :, RANK:]
        reduced = eye[None] - jnp.einsum("bij,bjk->bik", g_sib, g_own, precision=high)
        rhs = q_sib - jnp.einsum("bij,bjk->bik", g_sib, q_own, precision=high)
        solved = jax.vmap(eliminate)(reduced, rhs)
        panel = s_blocks[:RANK]
        others = s_blocks[RANK:] - jnp.einsum("bij,ibr->jbr", solved, panel, precision=high)
        stack = others.reshape(count - RANK, NTOT)
    return stack
```

```python
import jax
import jax.numpy as jnp
from jax import lax
from jax.experimental import pallas as pl
from jax.experimental.pallas import tpu as pltpu
from jax.sharding import PartitionSpec as P

LEVELS = 3
ROWS = 2048
COLS = 384
MESH = pl.DeviceIdType.MESH


def mm(a, b):
    return jnp.dot(a, b, precision=lax.Precision.HIGHEST, preferred_element_type=jnp.float32)


def swap(a):
    return pltpu.roll(a, 64, 1)


def low_lanes(rows):
    return lax.broadcasted_iota(jnp.int32, (rows, 128), 1) < 64


def pick(low, high):
    return jnp.where(low_lanes(low.shape[0]), low, high)


def eye_pair():
    row = lax.broadcasted_iota(jnp.int32, (64, 128), 0)
    lane = lax.broadcasted_iota(jnp.int32, (64, 128), 1)
    return jnp.where((lane == row) | (lane == row + 64), 1.0, 0.0).astype(jnp.float32)


def invert(start):
    row8 = lax.broadcasted_iota(jnp.int32, (8, 128), 0)

    def body(_, carry):
        top, rest = carry
        for first in (0, 4):
            tops = [jnp.broadcast_to(top[:, j : j + 1], (8, 128)) for j in range(first, first + 4)]
            rests = [jnp.broadcast_to(rest[:, j : j + 1], (56, 128)) for j in range(first, first + 4)]
            for step in range(4):
                k = first + step
                hit = row8 == k
                scale = 1.0 / tops[step][k : k + 1, :]
                line = top[k : k + 1, :] * scale
                top = jnp.where(hit, line, top - tops[step] * line)
                rest = rest - rests[step] * line
                for j in range(step + 1, 4):
                    part = tops[j][k : k + 1, :] * scale
                    tops[j] = jnp.where(hit, part, tops[j] - tops[step] * part)
                    rests[j] = rests[j] - rests[step] * part
        whole = pltpu.roll(jnp.concatenate([rest, top], axis=0), 120, 1)
        return whole[0:8], whole[8:64]

    top, rest = lax.fori_loop(0, 8, body, (start[0:8], start[8:64]))
    whole = jnp.concatenate([top, rest], axis=0)
    return pick(whole, swap(whole))


def solve_kernel(
    ranks_ref, len_ref, diag_ref, v_ref, u_ref, b_ref,
    tt_ref, uall_ref,
    vall, ub, lhs, stage, pair, chip, zbuf, hybuf, x1src, x1buf, x2buf, agsrc, agbuf,
    loc_sem, v_s, v_r, u_s, u_r, d_s, d_r, z_s, z_r, h_s, h_r, x1_s, x1_r, x2_s, x2_r, ag_s, ag_r, ad_s, ad_r,
):
    x = lax.axis_index("node")
    row = lax.axis_index("row")
    y = lax.axis_index("col")
    z = row // 2
    h = row % 2
    idx = y * 2 + h
    right = (x, row, (y + 1) % 4)
    left = (x, row, (y + 3) % 4)
    ypast = (y + 3) % 4
    ynext = (y + 1) % 4
    partner = (x, z * 2 + (1 - h), y)
    xnear = x + 1 - 2 * (x % 2)
    xfar = 2 * (1 - x // 2)
    block = z // 4

    def z_peer(d):
        return (x, ((z + d) % 8) * 2 + h, y)

    def h_peer(d):
        other = (idx + d) % 8
        return (x, z * 2 + other % 2, other // 2)

    def x_peer(d):
        return ((x + d) % 4, row, y)

    peers = [z_peer(d) for d in range(1, 8)] + [h_peer(d) for d in range(1, 8)] + [x_peer(d) for d in range(1, 4)]
    barrier = pltpu.get_barrier_semaphore()
    for peer in peers:
        pl.semaphore_signal(barrier, inc=1, device_id=peer, device_id_type=MESH)
    pl.semaphore_wait(barrier, len(peers))

    def remote(src, dst, send, recv, device):
        return pltpu.make_async_remote_copy(
            src_ref=src, dst_ref=dst, send_sem=send, recv_sem=recv, device_id=device, device_id_type=MESH
        )

    sent = []

    def go(copy):
        copy.start()
        sent.append(copy)

    def direct(src, dst, send, recv, l):
        return (
            remote(src.at[l], dst.at[l, y], send.at[l, 0], recv.at[l, 0], right),
            remote(src.at[l], dst.at[l, y], send.at[l, 1], recv.at[l, 1], left),
        )

    def onward(dst, send, recv, l):
        return (
            remote(dst.at[l, ypast, 0], dst.at[l, ypast, 0], send.at[l, 2], recv.at[l, 2], right),
            remote(dst.at[l, ynext, 1], dst.at[l, ynext, 1], send.at[l, 3], recv.at[l, 3], left),
        )

    v_direct = [direct(v_ref, vall, v_s, v_r, l) for l in range(LEVELS)]
    v_onward = [onward(vall, v_s, v_r, l) for l in range(LEVELS)]
    u_direct = [direct(u_ref, uall_ref, u_s, u_r, l) for l in range(LEVELS)]
    u_onward = [onward(uall_ref, u_s, u_r, l) for l in range(LEVELS)]

    def send_direct(copies, l):
        for copy in copies[l]:
            go(copy)

    def pass_on(direct_copies, onward_copies, l):
        for copy in direct_copies[l]:
            copy.wait_recv()
        for copy in onward_copies[l]:
            go(copy)

    send_direct(v_direct, 0)
    own_v = pltpu.make_async_copy(v_ref, vall.at[:, y], loc_sem.at[0])
    own_u = pltpu.make_async_copy(u_ref, ub, loc_sem.at[1])
    own_b = pltpu.make_async_copy(b_ref, lhs.at[0:COLS], loc_sem.at[2])
    keep_u = pltpu.make_async_copy(u_ref, uall_ref.at[:, y], loc_sem.at[3])
    own_v.start()
    own_u.start()
    own_b.start()
    keep_u.start()
    send_direct(v_direct, 1)

    weight = jnp.where(
        lax.broadcasted_iota(jnp.int32, (1, ROWS), 1) < len_ref[0], 1.0 / diag_ref[...], 0.0
    )
    own_u.wait()
    eight = lax.broadcasted_iota(jnp.int32, (8, 1), 0)
    parts = []
    for half in range(2):
        for l in range(LEVELS):
            kept = jnp.where(y * 16 + half * 8 + eight < ranks_ref[l], 1.0, 0.0)
            parts.append(ub[l, half] * kept)
    mine = jnp.concatenate(parts, axis=0)
    mine_hi = mine.astype(jnp.bfloat16)
    lhs[COLS : COLS + 48] = mine_hi
    lhs[COLS + 48 : COLS + 96] = (mine - mine_hi.astype(jnp.float32)).astype(jnp.bfloat16)
    own_v.wait()
    own_b.wait()

    def product(l):
        for copy in v_onward[l]:
            copy.wait_recv()
        kept = jnp.where(lax.broadcasted_iota(jnp.int32, (64, 1), 0) < ranks_ref[l], 1.0, 0.0)
        total = None
        for part in range(4):
            span = slice(512 * part, 512 * part + 512)
            scaled = vall[l, :, :, :, span].reshape(64, 512) * weight[:, span] * kept
            high = scaled.astype(jnp.bfloat16)
            low = (scaled - high.astype(jnp.float32)).astype(jnp.bfloat16)
            both = jnp.concatenate([high, low], axis=0)
            term = lax.dot_general(
                lhs[:, span], both, (((1,), (1,)), ((), ())), preferred_element_type=jnp.float32
            )
            total = term if total is None else total + term
        from_b = total[0:COLS]
        from_b = (from_b + swap(from_b)).reshape(2, 8, 24, 128)
        from_u = total[COLS : COLS + 48] + total[COLS + 48 : COLS + 96]
        from_u = (from_u + swap(from_u)).reshape(2, 1, 24, 128)
        lanes = lax.broadcasted_iota(jnp.int32, (2, 8, 24, 128), 3) < 64
        stage[l] = jnp.where(lanes, from_b, from_u)

    d_copies = [remote(stage.at[l, 1 - h], pair.at[l], d_s.at[l], d_r.at[l], partner) for l in range(LEVELS)]
    z_copies = [
        [remote(chip.at[l, (z + d) % 8], zbuf.at[l, z], z_s.at[l, d], z_r.at[l, d], z_peer(d)) for d in range(1, 8)]
        for l in range(LEVELS)
    ]
    h_copies = [
        [remote(hybuf.at[l, idx], hybuf.at[l, idx], h_s.at[l, d], h_r.at[l, d], h_peer(d)) for d in range(1, 8)]
        for l in range(LEVELS)
    ]

    def send_z(l):
        d_copies[l].wait_recv()
        chip[l] = stage[l, h] + pair[l]
        for copy in z_copies[l]:
            go(copy)
        zbuf[l, z] = chip[l, z]

    def send_h(l):
        for copy in z_copies[l]:
            copy.wait_recv()
        first = (zbuf[l, 0] + zbuf[l, 1]) + (zbuf[l, 2] + zbuf[l, 3])
        second = (zbuf[l, 4] + zbuf[l, 5]) + (zbuf[l, 6] + zbuf[l, 7])
        hybuf[l, idx] = pick(swap(first), second)
        for copy in h_copies[l]:
            go(copy)
        return pick(first, swap(second))

    def gathered(l, from_b):
        for copy in h_copies[l]:
            copy.wait_recv()
        panels = [hybuf[l, :, 8 * k : 8 * k + 8].reshape(64, 128) for k in range(LEVELS)]
        return panels[0], jnp.concatenate([panels[1], panels[2], from_b], axis=0)

    pass_on(v_direct, v_onward, 0)
    send_direct(v_direct, 2)
    product(0)
    go(d_copies[0])
    pass_on(v_direct, v_onward, 1)
    send_z(0)
    product(1)
    go(d_copies[1])
    b_0 = send_h(0)
    pass_on(v_direct, v_onward, 2)
    for l in range(LEVELS):
        send_direct(u_direct, l)
    send_z(1)

    panel, rhs = gathered(0, b_0)
    turned = swap(panel)
    inverse = invert(eye_pair() - mm(panel[:, :64], jnp.where(low_lanes(64), turned, 0.0)))

    product(2)
    go(d_copies[2])
    b_1 = send_h(1)
    send_z(2)

    rhs_turned = swap(rhs)
    first = mm(rhs_turned[:, :64] - mm(rhs[:, :64], turned[:, :64]), inverse)
    second = rhs_turned - mm(first[:, :64], pick(panel, turned))
    t0 = pick(first, second)

    def after_zero(l, from_b):
        lead, raw = gathered(l, from_b)
        lead_turned = swap(lead)
        stacked = jnp.concatenate([pick(lead, lead_turned), pick(lead_turned, lead)], axis=0)
        return raw + swap(raw) - mm(t0, stacked)

    w1 = after_zero(1, b_1)
    x1src[0:64] = pick(w1[0:64], w1[64:128])
    x1src[64:88] = w1[128:152]
    x1_copy = remote(x1src, x1buf, x1_s.at[0], x1_r.at[0], (xnear, row, y))
    go(x1_copy)
    b_2 = send_h(2)
    x1_copy.wait_recv()
    sib_panel = x1buf[0:64]
    sib_rhs = jnp.concatenate([swap(sib_panel), x1buf[64:88]], axis=0)
    inverse = invert(eye_pair() - mm(w1[0:64, :64], jnp.where(low_lanes(64), sib_panel, 0.0)))
    t1 = mm(sib_rhs[:, :64] - mm(w1[64:152, :64], sib_panel[:, :64]), inverse)

    agsrc[0] = pick(t0[128:152], t1[64:88])
    agsrc[1] = pick(swap(t0[128:152]), t1[64:88])
    ag0 = [
        remote(agsrc.at[((z + d) % 8) // 4], agbuf.at[0, h, z], ag_s.at[0, d], ag_r.at[0, d], z_peer(d))
        for d in range(1, 8)
    ]
    for copy in ag0:
        go(copy)
    agbuf[0, h, z] = agsrc[block]

    pass_on(u_direct, u_onward, 0)

    w2 = after_zero(2, b_2)
    x2buf[x] = w2[64:152] - mm(t1[:, :64], w2[0:64])
    x2_copies = [remote(x2buf.at[x], x2buf.at[x], x2_s.at[d], x2_r.at[d], x_peer(d)) for d in range(1, 4)]
    for copy in x2_copies:
        go(copy)
    for copy in ag0:
        copy.wait_recv()
    ad0 = remote(agbuf.at[0, h], agbuf.at[0, h], ad_s.at[0], ad_r.at[0], partner)
    go(ad0)
    pass_on(u_direct, u_onward, 1)
    for copy in x2_copies:
        copy.wait_recv()
    own = x2buf[x] + x2buf[xnear]
    sib = x2buf[xfar] + x2buf[xfar + 1]
    inverse = invert(eye_pair() - mm(own[0:64, :64], jnp.where(low_lanes(64), sib[0:64], 0.0)))
    t2 = mm(sib[64:88, :64] - mm(own[64:88, :64], sib[0:64, :64]), inverse)
    agbuf[1, h, z] = t2
    ag1 = [
        remote(agbuf.at[1, h, z], agbuf.at[1, h, z], ag_s.at[1, d], ag_r.at[1, d], z_peer(d)) for d in range(1, 8)
    ]
    for copy in ag1:
        go(copy)
    pass_on(u_direct, u_onward, 2)
    for copy in ag1:
        copy.wait_recv()
    ad1 = remote(agbuf.at[1, h], agbuf.at[1, h], ad_s.at[1], ad_r.at[1], partner)
    go(ad1)
    ad0.wait_recv()
    ad1.wait_recv()

    early = agbuf[0].reshape(COLS, 128)
    late = agbuf[1].reshape(COLS, 128)
    a_0 = jnp.where(block == 0, t0[0:128], swap(t0[0:128]))
    a_0 = pick(a_0, swap(a_0))
    c_1 = pick(swap(early), early) - mm(late[:, :64], t1[0:64])
    c_0 = early - mm(pick(c_1, late), a_0)
    lane = lax.broadcasted_iota(jnp.int32, (1, 128), 1)
    keep_01 = jnp.where(lane < jnp.where(lane < 64, ranks_ref[0], 64 + ranks_ref[1]), 1.0, 0.0)
    keep_2 = jnp.where(lane < ranks_ref[2], 1.0, 0.0)
    tt_ref[:, 0:128] = pick(c_0, c_1) * keep_01
    tt_ref[:, 128:256] = late * keep_2

    for l in range(LEVELS):
        for copy in u_onward[l]:
            copy.wait_recv()
    keep_u.wait()
    for copy in sent:
        copy.wait_send()


def final_kernel(width, len_ref, tt_ref, u_ref, b_ref, diag_ref, out_ref):
    coef = tt_ref[:, 0:192]
    coef_hi = coef.astype(jnp.bfloat16)
    coef_lo = (coef - coef_hi.astype(jnp.float32)).astype(jnp.bfloat16)
    panel = u_ref[...]
    panel_hi = panel.astype(jnp.bfloat16)
    panel_lo = (panel - panel_hi.astype(jnp.float32)).astype(jnp.bfloat16)

    def dot(a, b):
        return jnp.dot(a, b, preferred_element_type=jnp.float32)

    total = dot(coef_hi, panel_hi) + (dot(coef_lo, panel_hi) + dot(coef_hi, panel_lo))
    place = pl.program_id(0) * width + lax.broadcasted_iota(jnp.int32, (1, width), 1)
    live = place < len_ref[0]
    out_ref[...] = (b_ref[...].astype(jnp.float32) - jnp.where(live, total, 0.0)) * (1.0 / diag_ref[...])


def local(basis_u, basis_v, leaf_diag, right_side, leaf_len, ranks):
    f32 = jnp.float32
    diag = leaf_diag.reshape(1, ROWS)
    smem = pl.BlockSpec(memory_space=pltpu.SMEM)
    vmem = pl.BlockSpec(memory_space=pltpu.VMEM)
    hbm = pl.BlockSpec(memory_space=pl.ANY)
    dma = pltpu.SemaphoreType.DMA
    coef, panels = pl.pallas_call(
        solve_kernel,
        name="gather_and_solve",
        out_shape=(
            jax.ShapeDtypeStruct((COLS, 256), f32),
            jax.ShapeDtypeStruct((LEVELS, 4, 2, 8, ROWS), f32),
        ),
        in_specs=[smem, smem, vmem, hbm, hbm, hbm],
        out_specs=(vmem, hbm),
        scratch_shapes=[
            pltpu.VMEM((LEVELS, 4, 2, 8, ROWS), f32),
            pltpu.VMEM((LEVELS, 2, 8, ROWS), f32),
            pltpu.VMEM((COLS + 96, ROWS), jnp.bfloat16),
            pltpu.VMEM((LEVELS, 2, 8, 24, 128), f32),
            pltpu.VMEM((LEVELS, 8, 24, 128), f32),
            pltpu.VMEM((LEVELS, 8, 24, 128), f32),
            pltpu.VMEM((LEVELS, 8, 24, 128), f32),
            pltpu.VMEM((LEVELS, 8, 24, 128), f32),
            pltpu.VMEM((88, 128), f32),
            pltpu.VMEM((88, 128), f32),
            pltpu.VMEM((4, 88, 128), f32),
            pltpu.VMEM((2, 24, 128), f32),
            pltpu.VMEM((2, 2, 8, 24, 128), f32),
            dma((4,)),
            dma((LEVELS, 4)), dma((LEVELS, 4)),
            dma((LEVELS, 4)), dma((LEVELS, 4)),
            dma((LEVELS,)), dma((LEVELS,)),
            dma((LEVELS, 8)), dma((LEVELS, 8)),
            dma((LEVELS, 8)), dma((LEVELS, 8)),
            dma((1,)), dma((1,)),
            dma((4,)), dma((4,)),
            dma((2, 8)), dma((2, 8)),
            dma((2,)), dma((2,)),
        ],
        compiler_params=pltpu.CompilerParams(
            collective_id=0, has_side_effects=True, vmem_limit_bytes=32 * 1024 * 1024
        ),
    )(
        ranks,
        leaf_len,
        diag,
        basis_v.reshape(LEVELS, 2, 8, ROWS),
        basis_u.reshape(LEVELS, 2, 8, ROWS),
        right_side,
    )
    width = 512
    return pl.pallas_call(
        lambda *refs: final_kernel(width, *refs),
        name="correct_rows",
        grid=(ROWS // width,),
        out_shape=jax.ShapeDtypeStruct((COLS, ROWS), f32),
        in_specs=[
            smem,
            pl.BlockSpec((COLS, 256), lambda i: (0, 0)),
            pl.BlockSpec((192, width), lambda i: (0, i)),
            pl.BlockSpec((COLS, width), lambda i: (0, i)),
            pl.BlockSpec((1, width), lambda i: (0, i)),
        ],
        out_specs=pl.BlockSpec((COLS, width), lambda i: (0, i)),
        compiler_params=pltpu.CompilerParams(vmem_limit_bytes=32 * 1024 * 1024),
        cost_estimate=pl.CostEstimate(flops=2 * 3 * COLS * 192 * ROWS, bytes_accessed=6300000, transcendentals=0),
    )(leaf_len, coef, panels.reshape(192, ROWS), right_side, diag)


def solution(mesh):
    in_specs = (
        P(None, "col", ("node", "row")),
        P(None, "col", ("node", "row")),
        P(("node", "row")),
        P("col", ("node", "row")),
        P(("node", "row")),
        P(),
    )
    out_specs = P("col", ("node", "row"))
    return jax.shard_map(local, mesh=mesh, in_specs=in_specs, out_specs=out_specs, check_vma=False)
```

```python
import jax
import jax.numpy as jnp
from jax import lax
from jax.experimental import pallas as pl
from jax.experimental.pallas import tpu as pltpu
from jax.sharding import PartitionSpec as P

LEVELS = 3
ROWS = 2048
COLS = 384
MESH = pl.DeviceIdType.MESH


def split(a):
    high = a.astype(jnp.bfloat16)
    return high, (a - high.astype(jnp.float32)).astype(jnp.bfloat16)


def dot(a, b):
    return jnp.dot(a, b, preferred_element_type=jnp.float32)


def mm(a, b):
    high = a.astype(jnp.bfloat16).astype(jnp.float32)
    parts = pick(high, a - high).astype(jnp.bfloat16)
    left = jnp.concatenate([parts, high.astype(jnp.bfloat16)[:, :64]], axis=1)
    b_high, b_low = split(b)
    return dot(left, jnp.concatenate([b_high, b_high, b_low], axis=0))


def swap(a):
    return pltpu.roll(a, 64, 1)


def low_lanes(rows):
    return lax.broadcasted_iota(jnp.int32, (rows, 128), 1) < 64


def pick(low, high):
    return jnp.where(low_lanes(low.shape[0]), low, high)


def eye_pair():
    row = lax.broadcasted_iota(jnp.int32, (64, 128), 0)
    lane = lax.broadcasted_iota(jnp.int32, (64, 128), 1)
    return jnp.where((lane == row) | (lane == row + 64), 1.0, 0.0).astype(jnp.float32)


def invert(starts):
    row8 = lax.broadcasted_iota(jnp.int32, (8, 128), 0)

    def eight_steps(top, rest):
        for first in (0, 4):
            tops = [jnp.broadcast_to(top[:, j : j + 1], (8, 128)) for j in range(first, first + 4)]
            rests = [jnp.broadcast_to(rest[:, j : j + 1], (56, 128)) for j in range(first, first + 4)]
            for step in range(4):
                k = first + step
                hit = row8 == k
                scale = 1.0 / tops[step][k : k + 1, :]
                line = top[k : k + 1, :] * scale
                top = jnp.where(hit, line, top - tops[step] * line)
                rest = rest - rests[step] * line
                for j in range(step + 1, 4):
                    part = tops[j][k : k + 1, :] * scale
                    tops[j] = jnp.where(hit, part, tops[j] - tops[step] * part)
                    rests[j] = rests[j] - rests[step] * part
        whole = pltpu.roll(jnp.concatenate([rest, top], axis=0), 120, 1)
        return whole[0:8], whole[8:64]

    def body(_, carry):
        return tuple(eight_steps(*one) for one in carry)

    done = lax.fori_loop(0, 8, body, tuple((start[0:8], start[8:64]) for start in starts))
    wholes = [jnp.concatenate(one, axis=0) for one in done]
    return [pick(whole, swap(whole)) for whole in wholes]


def both(a):
    turned = swap(a)
    return pick(a, turned), pick(turned, a)


def eye_less(product):
    return eye_pair() - jnp.where(low_lanes(64), product, 0.0)


def solve_kernel(
    len_ref, ranks_in, diag_in, v_ref, u_ref, b_ref,
    sum_ref, left_ref, right_ref,
    ranks_ref, diag_ref, uall_ref, vall, lhs, stage, pair, chip, zbuf, ubuf, bbuf, agsrc, couple, first_t, second_t, early, late,
    loc_sem, v_s, v_r, u_s, u_r, d_s, d_r, z_s, z_r, h_s, h_r, b_s, b_r, e_s, e_r, ag_s, ag_r, ad_s, ad_r,
):
    x = lax.axis_index("node")
    row = lax.axis_index("row")
    y = lax.axis_index("col")
    own_v = pltpu.make_async_copy(v_ref, vall.at[:, y], loc_sem.at[0])
    own_u = pltpu.make_async_copy(u_ref, uall_ref.at[:, y], loc_sem.at[1])
    own_b = pltpu.make_async_copy(b_ref, lhs.at[0:COLS], loc_sem.at[2])
    small = [
        pltpu.make_async_copy(src, dst, loc_sem.at[3 + i])
        for i, (src, dst) in enumerate(((ranks_in, ranks_ref), (diag_in, diag_ref)))
    ]
    for copy in small + [own_u, own_v, own_b]:
        copy.start()
    z = row // 2
    h = row % 2
    right = (x, row, (y + 1) % 4)
    left = (x, row, (y + 3) % 4)
    ypast = (y + 3) % 4
    ynext = (y + 1) % 4
    partner = (x, z * 2 + (1 - h), y)
    block = z // 4

    def z_peer(d):
        return (x, ((z + d) % 8) * 2 + h, y)

    def plane_peer(d):
        return ((x + d // 4) % 4, row, (y + d % 4) % 4)

    peers = [partner] + [z_peer(d) for d in range(1, 8)] + [plane_peer(d) for d in range(1, 16)]
    barrier = pltpu.get_barrier_semaphore()
    for peer in peers:
        pl.semaphore_signal(barrier, inc=1, device_id=peer, device_id_type=MESH)
    pl.semaphore_wait(barrier, len(peers))

    def remote(src, dst, send, recv, device):
        return pltpu.make_async_remote_copy(
            src_ref=src, dst_ref=dst, send_sem=send, recv_sem=recv, device_id=device, device_id_type=MESH
        )

    sent = []

    def go(copy):
        copy.start()
        sent.append(copy)

    def direct(src, dst, send, recv, l):
        return (
            remote(src.at[l], dst.at[l, y], send.at[l, 0], recv.at[l, 0], right),
            remote(src.at[l], dst.at[l, y], send.at[l, 1], recv.at[l, 1], left),
        )

    def onward(dst, send, recv, l):
        return (
            remote(dst.at[l, ypast, 0], dst.at[l, ypast, 0], send.at[l, 2], recv.at[l, 2], right),
            remote(dst.at[l, ynext, 1], dst.at[l, ynext, 1], send.at[l, 3], recv.at[l, 3], left),
        )

    v_direct = [direct(v_ref, vall, v_s, v_r, l) for l in range(LEVELS)]
    v_onward = [onward(vall, v_s, v_r, l) for l in range(LEVELS)]
    u_direct = [direct(u_ref, uall_ref, u_s, u_r, l) for l in range(LEVELS)]
    u_onward = [onward(uall_ref, u_s, u_r, l) for l in range(LEVELS)]

    def send_direct(copies, l):
        for copy in copies[l]:
            go(copy)

    def pass_on(direct_copies, onward_copies, l):
        for copy in direct_copies[l]:
            copy.wait_recv()
        for copy in onward_copies[l]:
            go(copy)

    send_direct(v_direct, 0)
    send_direct(v_direct, 1)
    for copy in small:
        copy.wait()

    over = 1.0 / diag_ref[...]
    weight = jnp.where(lax.broadcasted_iota(jnp.int32, (1, ROWS), 1) < len_ref[0], over, 0.0)
    own_u.wait()
    eight = lax.broadcasted_iota(jnp.int32, (8, 1), 0)
    parts = []
    for half in range(2):
        for l in range(LEVELS):
            kept = jnp.where(y * 16 + half * 8 + eight < ranks_ref[l], 1.0, 0.0)
            parts.append(uall_ref[l, y, half] * kept)
    mine = jnp.concatenate(parts, axis=0)
    mine_hi = mine.astype(jnp.bfloat16)
    lhs[COLS : COLS + 48] = mine_hi
    lhs[COLS + 48 : COLS + 96] = (mine - mine_hi.astype(jnp.float32)).astype(jnp.bfloat16)
    own_v.wait()
    own_b.wait()

    def product(l):
        for copy in v_onward[l]:
            copy.wait_recv()
        kept = jnp.where(lax.broadcasted_iota(jnp.int32, (64, 1), 0) < ranks_ref[l], 1.0, 0.0)
        total = None
        for part in range(4):
            span = slice(512 * part, 512 * part + 512)
            scaled = vall[l, :, :, :, span].reshape(64, 512) * weight[:, span] * kept
            high = scaled.astype(jnp.bfloat16)
            low = (scaled - high.astype(jnp.float32)).astype(jnp.bfloat16)
            both = jnp.concatenate([high, low], axis=0)
            term = lax.dot_general(
                lhs[:, span], both, (((1,), (1,)), ((), ())), preferred_element_type=jnp.float32
            )
            total = term if total is None else total + term
        from_b = total[0:COLS]
        from_b = (from_b + swap(from_b)).reshape(2, 8, 24, 128)
        from_u = total[COLS : COLS + 48] + total[COLS + 48 : COLS + 96]
        from_u = (from_u + swap(from_u)).reshape(2, 1, 24, 128)
        lanes = lax.broadcasted_iota(jnp.int32, (2, 8, 24, 128), 3) < 64
        stage[l] = jnp.where(lanes, from_b, from_u)

    d_copies = [remote(stage.at[l, 1 - h], pair.at[l], d_s.at[l], d_r.at[l], partner) for l in range(LEVELS)]
    z_copies = [
        [remote(chip.at[l, (z + d) % 8], zbuf.at[l, z], z_s.at[l, d], z_r.at[l, d], z_peer(d)) for d in range(1, 8)]
        for l in range(LEVELS)
    ]
    plane_copies = [
        [
            remote(ubuf.at[l, h, x, y], ubuf.at[l, h, x, y], h_s.at[l, d], h_r.at[l, d], plane_peer(d))
            for d in range(1, 16)
        ]
        + [
            remote(bbuf.at[l, x], bbuf.at[l, x], b_s.at[l, d], b_r.at[l, d], plane_peer(4 * d))
            for d in range(1, 4)
        ]
        for l in range(LEVELS)
    ]
    share_copies = [remote(ubuf.at[l, h], ubuf.at[l, h], e_s.at[l], e_r.at[l], partner) for l in range(LEVELS)]

    def send_z(l):
        d_copies[l].wait_recv()
        chip[l] = stage[l, h] + pair[l]
        for copy in z_copies[l]:
            go(copy)
        zbuf[l, z] = chip[l, z]

    def send_plane(l):
        for copy in z_copies[l]:
            copy.wait_recv()
        first = (zbuf[l, 0] + zbuf[l, 1]) + (zbuf[l, 2] + zbuf[l, 3])
        second = (zbuf[l, 4] + zbuf[l, 5]) + (zbuf[l, 6] + zbuf[l, 7])
        ubuf[l, h, x, y] = pick(swap(first), second)
        bbuf[l, x] = pick(first, swap(second))
        for copy in plane_copies[l]:
            go(copy)

    def share(l):
        for copy in plane_copies[l]:
            copy.wait_recv()
        go(share_copies[l])

    def gathered(l, at):
        panels = [
            jnp.concatenate(
                [ubuf[l, half, at, col, 8 * k : 8 * k + 8] for col in range(4) for half in range(2)], axis=0
            )
            for k in range(LEVELS)
        ]
        return panels[0], jnp.concatenate([panels[1], panels[2], bbuf[l, at]], axis=0)

    pass_on(v_direct, v_onward, 0)
    send_direct(v_direct, 2)
    pass_on(v_direct, v_onward, 1)
    product(0)
    go(d_copies[0])
    send_z(0)
    pass_on(v_direct, v_onward, 2)
    product(1)
    go(d_copies[1])
    send_z(1)
    product(2)
    go(d_copies[2])
    send_z(2)
    send_plane(0)
    send_plane(1)
    share(0)
    send_plane(2)
    for l in range(LEVELS):
        send_direct(u_direct, l)
    share_copies[0].wait_recv()

    zero = [[both(part) for part in gathered(0, at)] for at in range(4)]
    inverse = invert([eye_less(mm(panel[0], panel[1])) for panel, _ in zero])
    share(1)
    t_low, t_high = [], []
    for at in range(4):
        (g_low, g_high), (q_low, q_high) = zero[at]
        t_low.append(mm(q_high - mm(q_low, g_high), inverse[at]))
        t_high.append(q_low - mm(t_low[at], g_low))
        first_t[at, 0] = t_low[at][0:128]
        first_t[at, 1] = t_high[at][0:128]
    share_copies[1].wait_recv()

    def after_zero(l, at):
        lead, raw = gathered(l, at)
        n_low, n_high = both(lead)
        return raw + swap(raw) - (mm(t_low[at], n_low) + mm(t_high[at], n_high))

    w1 = [after_zero(1, at) for at in range(4)]
    for at in range(4):
        sides = pick(w1[at // 2 * 2][128:152], w1[at // 2 * 2 + 1][128:152])
        for c, t in ((0, t_low[at]), (1, t_high[at])):
            agsrc[at, c, 0:24] = t[128:152]
            agsrc[at, c, 24:48] = sides
    early_copies = [
        remote(agsrc.at[x, ((z + d) % 8) // 4], early.at[h, z], ag_s.at[0, d], ag_r.at[0, d], z_peer(d))
        for d in range(1, 8)
    ]
    for copy in early_copies:
        go(copy)
    early[h, z] = agsrc[x, block]
    inverse = invert([eye_less(mm(w1[at][0:64], w1[at + 1][0:64])) for at in (0, 2)])
    share(2)
    pass_on(u_direct, u_onward, 0)
    t1 = []
    for even in (0, 2):
        low, high = w1[even], w1[even + 1]
        one = mm(high[64:152] - mm(low[64:152], high[0:64]), inverse[even // 2])
        t1 += [one, low[64:152] - mm(one, low[0:64])]
        couple[even // 2, 0] = low[0:64]
        couple[even // 2, 1] = high[0:64]
        couple[even // 2, 2] = inverse[even // 2]
    for at in range(4):
        second_t[at] = t1[at][0:64]
    share_copies[2].wait_recv()

    w2 = [after_zero(2, at) for at in range(4)]
    p2 = [w2[at][64:152] - mm(t1[at], w2[at][0:64]) for at in range(4)]
    low, high = p2[0] + p2[1], p2[2] + p2[3]
    own = jnp.where(x < 2, low, high)
    sib = jnp.where(x < 2, high, low)
    late[h, z] = pick(own[64:88], sib[64:88])
    late_copies = [
        remote(late.at[h, z], late.at[h, z], ag_s.at[1, d], ag_r.at[1, d], z_peer(d)) for d in range(1, 8)
    ]
    for copy in late_copies:
        go(copy)
    pass_on(u_direct, u_onward, 1)
    pass_on(u_direct, u_onward, 2)
    (inverse,) = invert([eye_less(mm(own[0:64], sib[0:64]))])
    for copy in early_copies:
        copy.wait_recv()
    early_share = remote(early.at[h], early.at[h], ad_s.at[0], ad_r.at[0], partner)
    go(early_share)

    a_01 = first_t[x, block, 0:64]
    a_02 = first_t[x, block, 64:128]
    a_12 = second_t[x]
    c_1 = mm(inverse, a_12)
    c_0 = mm(inverse, a_02) - mm(c_1, a_01)
    last_01 = -pick(c_0, c_1)
    last_2 = inverse[:, :64]
    early_share.wait_recv()
    t_0 = early[:, :, 0:24].reshape(COLS, 128)
    q_even, q_odd = both(early[:, :, 24:48].reshape(COLS, 128))
    t_even = mm(q_odd - mm(q_even, couple[x // 2, 1]), couple[x // 2, 2])
    t_odd = q_even - mm(t_even, couple[x // 2, 0])
    t_1 = jnp.where(x % 2 == 0, t_even, t_odd)
    t_0 = t_0 - mm(t_1, a_01)
    front_high, front_low = split(pick(t_0, t_1))
    last_high, last_low = split(jnp.concatenate([last_01, last_2], axis=1))
    for l in range(LEVELS):
        for copy in u_onward[l]:
            copy.wait_recv()
    place = lax.broadcasted_iota(jnp.int32, (64, 1), 0)
    kept = jnp.concatenate([jnp.where(place < ranks_ref[l], 1.0, 0.0) for l in range(LEVELS)], axis=0)
    for part in range(4):
        span = slice(512 * part, 512 * part + 512)
        panel_high, panel_low = split(uall_ref[:, :, :, :, span].reshape(192, 512) * kept)
        last = dot(last_high, panel_high) + (dot(last_low, panel_high) + dot(last_high, panel_low))
        last_h, last_l = split(last * weight[:, span])
        right_ref[0:64, span] = last_h
        right_ref[64:128, span] = last_h
        right_ref[128:192, span] = last_l
        front = dot(front_high, panel_high[0:128]) + (
            dot(front_low, panel_high[0:128]) + dot(front_high, panel_low[0:128])
        )
        sum_ref[:, span] = lhs[0:COLS, span].astype(jnp.float32) * over[:, span] - front * weight[:, span]

    for copy in late_copies:
        copy.wait_recv()
    late_share = remote(late.at[h], late.at[h], ad_s.at[1], ad_r.at[1], partner)
    go(late_share)
    late_share.wait_recv()
    q_own, q_sib = both(late[...].reshape(COLS, 128))
    rest = q_sib - mm(q_own, sib[0:64])
    rest_high = rest.astype(jnp.bfloat16).astype(jnp.float32)
    left_ref[:, 0:128] = pick(rest_high, rest - rest_high).astype(jnp.bfloat16)
    left_ref[:, 128:192] = rest_high.astype(jnp.bfloat16)[:, :64]

    for copy in sent:
        copy.wait_send()


def final_kernel(sum_ref, left_ref, right_ref, out_ref):
    out_ref[...] = sum_ref[...] - dot(left_ref[...], right_ref[...])


def local(basis_u, basis_v, leaf_diag, right_side, leaf_len, ranks):
    f32 = jnp.float32
    diag = leaf_diag.reshape(1, ROWS)
    vmem = pl.BlockSpec(memory_space=pltpu.VMEM)
    dma = pltpu.SemaphoreType.DMA
    total, left, right = pl.pallas_call(
        solve_kernel,
        name="gather_and_solve",
        out_shape=(
            pltpu.VMEM((COLS, ROWS), f32),
            pltpu.VMEM((COLS, 192), jnp.bfloat16),
            pltpu.VMEM((192, ROWS), jnp.bfloat16),
        ),
        in_specs=[pl.BlockSpec(memory_space=pltpu.SMEM)] + [pl.BlockSpec(memory_space=pltpu.HBM)] * 5,
        out_specs=(vmem, vmem, vmem),
        scratch_shapes=[
            pltpu.SMEM((LEVELS,), jnp.int32),
            pltpu.VMEM((1, ROWS), f32),
            pltpu.VMEM((LEVELS, 4, 2, 8, ROWS), f32),
            pltpu.VMEM((LEVELS, 4, 2, 8, ROWS), f32),
            pltpu.VMEM((COLS + 96, ROWS), jnp.bfloat16),
            pltpu.VMEM((LEVELS, 2, 8, 24, 128), f32),
            pltpu.VMEM((LEVELS, 8, 24, 128), f32),
            pltpu.VMEM((LEVELS, 8, 24, 128), f32),
            pltpu.VMEM((LEVELS, 8, 24, 128), f32),
            pltpu.VMEM((LEVELS, 2, 4, 4, 24, 128), f32),
            pltpu.VMEM((LEVELS, 4, 24, 128), f32),
            pltpu.VMEM((4, 2, 48, 128), f32),
            pltpu.VMEM((2, 3, 64, 128), f32),
            pltpu.VMEM((4, 2, 128, 128), f32),
            pltpu.VMEM((4, 64, 128), f32),
            pltpu.VMEM((2, 8, 48, 128), f32),
            pltpu.VMEM((2, 8, 24, 128), f32),
            dma((5,)),
            dma((LEVELS, 4)), dma((LEVELS, 4)),
            dma((LEVELS, 4)), dma((LEVELS, 4)),
            dma((LEVELS,)), dma((LEVELS,)),
            dma((LEVELS, 8)), dma((LEVELS, 8)),
            dma((LEVELS, 16)), dma((LEVELS, 16)),
            dma((LEVELS, 4)), dma((LEVELS, 4)),
            dma((LEVELS,)), dma((LEVELS,)),
            dma((2, 8)), dma((2, 8)),
            dma((2,)), dma((2,)),
        ],
        compiler_params=pltpu.CompilerParams(
            collective_id=0, has_side_effects=True, vmem_limit_bytes=40 * 1024 * 1024
        ),
    )(
        leaf_len,
        *[
            pltpu.with_memory_space_constraint(array, pltpu.HBM)
            for array in (
                ranks,
                diag,
                basis_v.reshape(LEVELS, 2, 8, ROWS),
                basis_u.reshape(LEVELS, 2, 8, ROWS),
                right_side,
            )
        ]
    )
    width = 512
    return pl.pallas_call(
        final_kernel,
        name="add_last_panel",
        grid=(ROWS // width,),
        out_shape=jax.ShapeDtypeStruct((COLS, ROWS), f32),
        in_specs=[
            pl.BlockSpec((COLS, width), lambda i: (0, i)),
            pl.BlockSpec((COLS, 192), lambda i: (0, 0)),
            pl.BlockSpec((192, width), lambda i: (0, i)),
        ],
        out_specs=pl.BlockSpec((COLS, width), lambda i: (0, i)),
        compiler_params=pltpu.CompilerParams(vmem_limit_bytes=32 * 1024 * 1024),
        cost_estimate=pl.CostEstimate(flops=2 * COLS * 192 * ROWS, bytes_accessed=7200000, transcendentals=0),
    )(total, left, right)


def solution(mesh):
    in_specs = (
        P(None, "col", ("node", "row")),
        P(None, "col", ("node", "row")),
        P(("node", "row")),
        P("col", ("node", "row")),
        P(("node", "row")),
        P(),
    )
    out_specs = P("col", ("node", "row"))
    return jax.shard_map(local, mesh=mesh, in_specs=in_specs, out_specs=out_specs, check_vma=False)
```

```python
import functools

import jax
import jax.numpy as jnp
from jax import lax
from jax.experimental import pallas as pl
from jax.experimental.pallas import tpu as pltpu
from jax.sharding import PartitionSpec as P

LEVELS = 3
ROWS = 2048
COLS = 384
MESH = pl.DeviceIdType.MESH


def split(a):
    high = a.astype(jnp.bfloat16)
    return high, (a - high.astype(jnp.float32)).astype(jnp.bfloat16)


def dot(a, b):
    return jnp.dot(a, b, preferred_element_type=jnp.float32)


def mm(a, b):
    high = a.astype(jnp.bfloat16).astype(jnp.float32)
    parts = pick(high, a - high).astype(jnp.bfloat16)
    left = jnp.concatenate([parts, high.astype(jnp.bfloat16)[:, :64]], axis=1)
    b_high, b_low = split(b)
    return dot(left, jnp.concatenate([b_high, b_high, b_low], axis=0))


def swap(a):
    return pltpu.roll(a, 64, 1)


def low_lanes(rows):
    return lax.broadcasted_iota(jnp.int32, (rows, 128), 1) < 64


def pick(low, high):
    return jnp.where(low_lanes(low.shape[0]), low, high)


def eye_pair():
    row = lax.broadcasted_iota(jnp.int32, (64, 128), 0)
    lane = lax.broadcasted_iota(jnp.int32, (64, 128), 1)
    return jnp.where((lane == row) | (lane == row + 64), 1.0, 0.0).astype(jnp.float32)


def invert(starts):
    row8 = lax.broadcasted_iota(jnp.int32, (8, 128), 0)

    def eight_steps(top, rest):
        for first in (0, 4):
            tops = [jnp.broadcast_to(top[:, j : j + 1], (8, 128)) for j in range(first, first + 4)]
            rests = [jnp.broadcast_to(rest[:, j : j + 1], (56, 128)) for j in range(first, first + 4)]
            for step in range(4):
                k = first + step
                hit = row8 == k
                scale = 1.0 / tops[step][k : k + 1, :]
                line = top[k : k + 1, :] * scale
                top = jnp.where(hit, line, top - tops[step] * line)
                rest = rest - rests[step] * line
                for j in range(step + 1, 4):
                    part = tops[j][k : k + 1, :] * scale
                    tops[j] = jnp.where(hit, part, tops[j] - tops[step] * part)
                    rests[j] = rests[j] - rests[step] * part
        whole = pltpu.roll(jnp.concatenate([rest, top], axis=0), 120, 1)
        return whole[0:8], whole[8:64]

    def body(_, carry):
        return tuple(eight_steps(*one) for one in carry)

    done = lax.fori_loop(0, 8, body, tuple((start[0:8], start[8:64]) for start in starts))
    wholes = [jnp.concatenate(one, axis=0) for one in done]
    return [pick(whole, swap(whole)) for whole in wholes]


def both(a):
    turned = swap(a)
    return pick(a, turned), pick(turned, a)


def eye_less(product):
    return eye_pair() - jnp.where(low_lanes(64), product, 0.0)


def solve_kernel(
    len_ref, ranks_in, diag_in, v_ref, u_ref, b_ref,
    sum_ref, left_ref, right_ref,
    ranks_ref, diag_ref, uall_ref, vall, lhs, stage, pair, chip, zbuf, ubuf, bbuf, agsrc, couple, first_t, second_t, early, late,
    loc_sem, v_s, v_r, u_s, u_r, d_s, d_r, z_s, z_r, h_s, h_r, b_s, b_r, e_s, e_r, ag_s, ag_r, ad_s, ad_r,
):
    x = lax.axis_index("node")
    row = lax.axis_index("row")
    y = lax.axis_index("col")
    own_v = pltpu.make_async_copy(v_ref, vall.at[:, y], loc_sem.at[0])
    own_u = pltpu.make_async_copy(u_ref, uall_ref.at[:, y], loc_sem.at[1])
    own_b = pltpu.make_async_copy(b_ref, lhs.at[0:COLS], loc_sem.at[2])
    small = [
        pltpu.make_async_copy(src, dst, loc_sem.at[3 + i])
        for i, (src, dst) in enumerate(((ranks_in, ranks_ref), (diag_in, diag_ref)))
    ]
    for copy in small + [own_u, own_v, own_b]:
        copy.start()
    z = row // 2
    h = row % 2
    right = (x, row, (y + 1) % 4)
    left = (x, row, (y + 3) % 4)
    ypast = (y + 3) % 4
    ynext = (y + 1) % 4
    partner = (x, z * 2 + (1 - h), y)
    block = z // 4

    def z_peer(d):
        return (x, ((z + d) % 8) * 2 + h, y)

    def core_peer(d):
        return (x, (row + d) % 16, y)

    def plane_peer(d):
        return ((x + d // 4) % 4, row, (y + d % 4) % 4)

    peers = [core_peer(d) for d in range(1, 16)] + [plane_peer(d) for d in range(1, 16)]
    barrier = pltpu.get_barrier_semaphore()
    for peer in peers:
        pl.semaphore_signal(barrier, inc=1, device_id=peer, device_id_type=MESH)
    for copy in small:
        copy.wait()
    over = 1.0 / diag_ref[...]
    weight = jnp.where(lax.broadcasted_iota(jnp.int32, (1, ROWS), 1) < len_ref[0], over, 0.0)
    own_u.wait()
    eight = lax.broadcasted_iota(jnp.int32, (8, 1), 0)
    parts = []
    for half in range(2):
        for l in range(LEVELS):
            kept = jnp.where(y * 16 + half * 8 + eight < ranks_ref[l], 1.0, 0.0)
            parts.append(uall_ref[l, y, half] * kept)
    mine = jnp.concatenate(parts, axis=0)
    mine_hi = mine.astype(jnp.bfloat16)
    lhs[COLS : COLS + 48] = mine_hi
    lhs[COLS + 48 : COLS + 96] = (mine - mine_hi.astype(jnp.float32)).astype(jnp.bfloat16)
    pl.semaphore_wait(barrier, len(peers))

    def remote(src, dst, send, recv, device):
        return pltpu.make_async_remote_copy(
            src_ref=src, dst_ref=dst, send_sem=send, recv_sem=recv, device_id=device, device_id_type=MESH
        )

    sent = []

    def go(copy):
        copy.start()
        sent.append(copy)

    def start_all(copies):
        for copy in copies:
            copy.start()

    def wait_all(whole, sem):
        pltpu.make_async_copy(whole, whole, sem).wait()

    def direct(src, dst, send, recv, l):
        return (
            remote(src.at[l], dst.at[l, y], send.at[l, 0], recv.at[l, 0], right),
            remote(src.at[l], dst.at[l, y], send.at[l, 1], recv.at[l, 1], left),
        )

    def onward(dst, send, recv, l):
        return (
            remote(dst.at[l, ypast, 0], dst.at[l, ypast, 0], send.at[l, 2], recv.at[l, 2], right),
            remote(dst.at[l, ynext, 1], dst.at[l, ynext, 1], send.at[l, 3], recv.at[l, 3], left),
        )

    v_direct = [direct(v_ref, vall, v_s, v_r, l) for l in range(LEVELS)]
    v_onward = [onward(vall, v_s, v_r, l) for l in range(LEVELS)]
    u_direct = [direct(u_ref, uall_ref, u_s, u_r, l) for l in range(LEVELS)]
    u_onward = [onward(uall_ref, u_s, u_r, l) for l in range(LEVELS)]

    def send_direct(copies, l):
        for copy in copies[l]:
            go(copy)

    def pass_on(direct_copies, onward_copies, l):
        for copy in direct_copies[l]:
            copy.wait_recv()
        for copy in onward_copies[l]:
            go(copy)

    send_direct(v_direct, 0)
    send_direct(v_direct, 1)
    own_v.wait()
    own_b.wait()

    def product(l):
        for copy in v_onward[l]:
            copy.wait_recv()
        kept = jnp.where(lax.broadcasted_iota(jnp.int32, (64, 1), 0) < ranks_ref[l], 1.0, 0.0)
        total = None
        for part in range(4):
            span = slice(512 * part, 512 * part + 512)
            scaled = vall[l, :, :, :, span].reshape(64, 512) * weight[:, span] * kept
            high = scaled.astype(jnp.bfloat16)
            low = (scaled - high.astype(jnp.float32)).astype(jnp.bfloat16)
            both = jnp.concatenate([high, low], axis=0)
            term = lax.dot_general(
                lhs[:, span], both, (((1,), (1,)), ((), ())), preferred_element_type=jnp.float32
            )
            total = term if total is None else total + term
        from_b = total[0:COLS]
        from_b = (from_b + swap(from_b)).reshape(2, 8, 24, 128)
        from_u = total[COLS : COLS + 48] + total[COLS + 48 : COLS + 96]
        from_u = (from_u + swap(from_u)).reshape(2, 1, 24, 128)
        lanes = lax.broadcasted_iota(jnp.int32, (2, 8, 24, 128), 3) < 64
        stage[l] = jnp.where(lanes, from_b, from_u)

    d_copies = [remote(stage.at[l, 1 - h], pair.at[l], d_s.at[l], d_r.at[l], partner) for l in range(LEVELS)]
    z_copies = [
        [remote(chip.at[l, (z + d) % 8], zbuf.at[l, z], z_s.at[l], z_r.at[l], z_peer(d)) for d in range(1, 8)]
        for l in range(LEVELS)
    ]
    spot = x * 4 + y
    u_copies = [
        [remote(ubuf.at[l, h, spot], ubuf.at[l, h, spot], h_s.at[l], h_r.at[l], plane_peer(d)) for d in range(1, 16)]
        for l in range(LEVELS)
    ]
    b_copies = [
        [remote(bbuf.at[l, x], bbuf.at[l, x], b_s.at[l], b_r.at[l], plane_peer(4 * d)) for d in range(1, 4)]
        for l in range(LEVELS)
    ]
    share_copies = [remote(ubuf.at[l, h], ubuf.at[l, h], e_s.at[l], e_r.at[l], partner) for l in range(LEVELS)]

    def send_z(l):
        d_copies[l].wait_recv()
        chip[l] = stage[l, h] + pair[l]
        start_all(z_copies[l])
        zbuf[l, z] = chip[l, z]

    def send_plane(l):
        wait_all(zbuf.at[l, 0:7], z_r.at[l])
        first = (zbuf[l, 0] + zbuf[l, 1]) + (zbuf[l, 2] + zbuf[l, 3])
        second = (zbuf[l, 4] + zbuf[l, 5]) + (zbuf[l, 6] + zbuf[l, 7])
        ubuf[l, h, spot] = pick(swap(first), second)
        bbuf[l, x] = pick(first, swap(second))
        start_all(u_copies[l])
        start_all(b_copies[l])

    def share(l):
        wait_all(ubuf.at[l, h, 0:15], h_r.at[l])
        wait_all(bbuf.at[l, 0:3], b_r.at[l])
        go(share_copies[l])

    def gathered(l, at):
        panels = [
            jnp.concatenate(
                [ubuf[l, half, 4 * at + col, 8 * k : 8 * k + 8] for col in range(4) for half in range(2)], axis=0
            )
            for k in range(LEVELS)
        ]
        return panels[0], jnp.concatenate([panels[1], panels[2], bbuf[l, at]], axis=0)

    pass_on(v_direct, v_onward, 0)
    send_direct(v_direct, 2)
    pass_on(v_direct, v_onward, 1)
    product(0)
    go(d_copies[0])
    send_z(0)
    pass_on(v_direct, v_onward, 2)
    product(1)
    go(d_copies[1])
    send_z(1)
    product(2)
    go(d_copies[2])
    send_z(2)
    send_plane(0)
    send_plane(1)
    share(0)
    send_plane(2)
    for l in range(LEVELS):
        send_direct(u_direct, l)
    share_copies[0].wait_recv()

    zero = [[both(part) for part in gathered(0, at)] for at in range(4)]
    inverse = invert([eye_less(mm(panel[0], panel[1])) for panel, _ in zero])
    share(1)
    t_low, t_high = [], []
    for at in range(4):
        (g_low, g_high), (q_low, q_high) = zero[at]
        t_low.append(mm(q_high - mm(q_low, g_high), inverse[at]))
        t_high.append(q_low - mm(t_low[at], g_low))
        first_t[at, 0] = t_low[at][0:128]
        first_t[at, 1] = t_high[at][0:128]
    share_copies[1].wait_recv()

    def after_zero(l, at):
        lead, raw = gathered(l, at)
        n_low, n_high = both(lead)
        return raw + swap(raw) - (mm(t_low[at], n_low) + mm(t_high[at], n_high))

    w1 = [after_zero(1, at) for at in range(4)]
    for at in range(4):
        sides = pick(w1[at // 2 * 2][128:152], w1[at // 2 * 2 + 1][128:152])
        for c, t in ((0, t_low[at]), (1, t_high[at])):
            agsrc[at, c, 0:24] = t[128:152]
            agsrc[at, c, 24:48] = sides
    early_copies = [
        remote(agsrc.at[x, ((z + d) % 8) // 4], early.at[h, z], ag_s.at[0], ag_r.at[0], z_peer(d))
        for d in range(1, 8)
    ]
    start_all(early_copies)
    early[h, z] = agsrc[x, block]
    inverse = invert([eye_less(mm(w1[at][0:64], w1[at + 1][0:64])) for at in (0, 2)])
    share(2)
    pass_on(u_direct, u_onward, 0)
    t1 = []
    for even in (0, 2):
        low, high = w1[even], w1[even + 1]
        one = mm(high[64:152] - mm(low[64:152], high[0:64]), inverse[even // 2])
        t1 += [one, low[64:152] - mm(one, low[0:64])]
        couple[even // 2, 0] = low[0:64]
        couple[even // 2, 1] = high[0:64]
        couple[even // 2, 2] = inverse[even // 2]
    for at in range(4):
        second_t[at] = t1[at][0:64]
    share_copies[2].wait_recv()

    w2 = [after_zero(2, at) for at in range(4)]
    p2 = [w2[at][64:152] - mm(t1[at], w2[at][0:64]) for at in range(4)]
    low, high = p2[0] + p2[1], p2[2] + p2[3]
    own = jnp.where(x < 2, low, high)
    sib = jnp.where(x < 2, high, low)
    late[h * 8 + z] = pick(own[64:88], sib[64:88])
    late_copies = [
        remote(late.at[h * 8 + z], late.at[h * 8 + z], ag_s.at[1], ag_r.at[1], core_peer(d)) for d in range(1, 16)
    ]
    start_all(late_copies)
    pass_on(u_direct, u_onward, 1)
    pass_on(u_direct, u_onward, 2)
    (inverse,) = invert([eye_less(mm(own[0:64], sib[0:64]))])
    wait_all(early.at[h, 0:7], ag_r.at[0])
    early_share = remote(early.at[h], early.at[h], ad_s.at[0], ad_r.at[0], partner)
    go(early_share)

    a_01 = first_t[x, block, 0:64]
    a_02 = first_t[x, block, 64:128]
    a_12 = second_t[x]
    c_1 = mm(inverse, a_12)
    c_0 = mm(inverse, a_02) - mm(c_1, a_01)
    last_01 = -pick(c_0, c_1)
    last_2 = inverse[:, :64]
    early_share.wait_recv()
    t_0 = early[:, :, 0:24].reshape(COLS, 128)
    q_even, q_odd = both(early[:, :, 24:48].reshape(COLS, 128))
    t_even = mm(q_odd - mm(q_even, couple[x // 2, 1]), couple[x // 2, 2])
    t_odd = q_even - mm(t_even, couple[x // 2, 0])
    t_1 = jnp.where(x % 2 == 0, t_even, t_odd)
    t_0 = t_0 - mm(t_1, a_01)
    front_high, front_low = split(pick(t_0, t_1))
    last_high, last_low = split(jnp.concatenate([last_01, last_2], axis=1))
    for l in range(LEVELS):
        for copy in u_onward[l]:
            copy.wait_recv()
    place = lax.broadcasted_iota(jnp.int32, (64, 1), 0)
    kept = jnp.concatenate([jnp.where(place < ranks_ref[l], 1.0, 0.0) for l in range(LEVELS)], axis=0)
    for part in range(4):
        span = slice(512 * part, 512 * part + 512)
        panel_high, panel_low = split(uall_ref[:, :, :, :, span].reshape(192, 512) * kept)
        last = dot(last_high, panel_high) + (dot(last_low, panel_high) + dot(last_high, panel_low))
        last_h, last_l = split(last * weight[:, span])
        right_ref[0:64, span] = last_h
        right_ref[64:128, span] = last_h
        right_ref[128:192, span] = last_l
        front = dot(front_high, panel_high[0:128]) + (
            dot(front_low, panel_high[0:128]) + dot(front_high, panel_low[0:128])
        )
        sum_ref[:, span] = lhs[0:COLS, span].astype(jnp.float32) * over[:, span] - front * weight[:, span]

    for copy in sent:
        copy.wait_send()
    for l in range(LEVELS):
        wait_all(chip.at[l, 0:7], z_s.at[l])
        wait_all(ubuf.at[l, h, 0:15], h_s.at[l])
        wait_all(bbuf.at[l, 0:3], b_s.at[l])
    wait_all(early.at[h, 0:7], ag_s.at[0])
    wait_all(late.at[0:15], ag_r.at[1])
    q_own, q_sib = both(late[...].reshape(COLS, 128))
    rest = q_sib - mm(q_own, sib[0:64])
    rest_high = rest.astype(jnp.bfloat16).astype(jnp.float32)
    left_ref[:, 0:128] = pick(rest_high, rest - rest_high).astype(jnp.bfloat16)
    left_ref[:, 128:192] = rest_high.astype(jnp.bfloat16)[:, :64]

    wait_all(late.at[0:15], ag_s.at[1])


def final_kernel(width, sum_ref, left_ref, right_ref, out_ref):
    span = pl.ds(pl.multiple_of(pl.program_id(0) * width, width), width)
    out_ref[...] = sum_ref[:, span] - dot(left_ref[...], right_ref[:, span])


def local(basis_u, basis_v, leaf_diag, right_side, leaf_len, ranks):
    f32 = jnp.float32
    diag = leaf_diag.reshape(1, ROWS)
    vmem = pl.BlockSpec(memory_space=pltpu.VMEM)
    dma = pltpu.SemaphoreType.DMA
    total, left, right = pl.pallas_call(
        solve_kernel,
        name="gather_and_solve",
        out_shape=(
            pltpu.VMEM((COLS, ROWS), f32),
            pltpu.VMEM((COLS, 192), jnp.bfloat16),
            pltpu.VMEM((192, ROWS), jnp.bfloat16),
        ),
        in_specs=[pl.BlockSpec(memory_space=pltpu.SMEM)] + [pl.BlockSpec(memory_space=pltpu.HBM)] * 5,
        out_specs=(vmem, vmem, vmem),
        scratch_shapes=[
            pltpu.SMEM((LEVELS,), jnp.int32),
            pltpu.VMEM((1, ROWS), f32),
            pltpu.VMEM((LEVELS, 4, 2, 8, ROWS), f32),
            pltpu.VMEM((LEVELS, 4, 2, 8, ROWS), f32),
            pltpu.VMEM((COLS + 96, ROWS), jnp.bfloat16),
            pltpu.VMEM((LEVELS, 2, 8, 24, 128), f32),
            pltpu.VMEM((LEVELS, 8, 24, 128), f32),
            pltpu.VMEM((LEVELS, 8, 24, 128), f32),
            pltpu.VMEM((LEVELS, 8, 24, 128), f32),
            pltpu.VMEM((LEVELS, 2, 16, 24, 128), f32),
            pltpu.VMEM((LEVELS, 4, 24, 128), f32),
            pltpu.VMEM((4, 2, 48, 128), f32),
            pltpu.VMEM((2, 3, 64, 128), f32),
            pltpu.VMEM((4, 2, 128, 128), f32),
            pltpu.VMEM((4, 64, 128), f32),
            pltpu.VMEM((2, 8, 48, 128), f32),
            pltpu.VMEM((16, 24, 128), f32),
            dma((5,)),
            dma((LEVELS, 4)), dma((LEVELS, 4)),
            dma((LEVELS, 4)), dma((LEVELS, 4)),
            dma((LEVELS,)), dma((LEVELS,)),
            dma((LEVELS,)), dma((LEVELS,)),
            dma((LEVELS,)), dma((LEVELS,)),
            dma((LEVELS,)), dma((LEVELS,)),
            dma((LEVELS,)), dma((LEVELS,)),
            dma((2,)), dma((2,)),
            dma((1,)), dma((1,)),
        ],
        compiler_params=pltpu.CompilerParams(
            collective_id=0, has_side_effects=True, vmem_limit_bytes=40 * 1024 * 1024
        ),
    )(
        leaf_len,
        *[
            pltpu.with_memory_space_constraint(array, pltpu.HBM)
            for array in (
                ranks,
                diag,
                basis_v.reshape(LEVELS, 2, 8, ROWS),
                basis_u.reshape(LEVELS, 2, 8, ROWS),
                right_side,
            )
        ]
    )
    width = 512
    return pl.pallas_call(
        functools.partial(final_kernel, width),
        name="add_last_panel",
        grid=(ROWS // width,),
        out_shape=jax.ShapeDtypeStruct((COLS, ROWS), f32),
        in_specs=[vmem, vmem, vmem],
        out_specs=pl.BlockSpec((COLS, width), lambda i: (0, i)),
        compiler_params=pltpu.CompilerParams(vmem_limit_bytes=32 * 1024 * 1024),
        cost_estimate=pl.CostEstimate(flops=2 * COLS * 192 * ROWS, bytes_accessed=7200000, transcendentals=0),
    )(total, left, right)


def solution(mesh):
    in_specs = (
        P(None, "col", ("node", "row")),
        P(None, "col", ("node", "row")),
        P(("node", "row")),
        P("col", ("node", "row")),
        P(("node", "row")),
        P(),
    )
    out_specs = P("col", ("node", "row"))
    return jax.shard_map(local, mesh=mesh, in_specs=in_specs, out_specs=out_specs, check_vma=False)
```

```python
import functools

import jax
import jax.numpy as jnp
from jax import lax
from jax.experimental import pallas as pl
from jax.experimental.pallas import tpu as pltpu
from jax.sharding import PartitionSpec as P

LEVELS = 3
ROWS = 2048
COLS = 384
MESH = pl.DeviceIdType.MESH


def split(a):
    high = a.astype(jnp.bfloat16)
    return high, (a - high.astype(jnp.float32)).astype(jnp.bfloat16)


def dot(a, b):
    return jnp.dot(a, b, preferred_element_type=jnp.float32)


def mm(a, b):
    high = a.astype(jnp.bfloat16).astype(jnp.float32)
    parts = pick(high, a - high).astype(jnp.bfloat16)
    left = jnp.concatenate([parts, high.astype(jnp.bfloat16)[:, :64]], axis=1)
    b_high, b_low = split(b)
    return dot(left, jnp.concatenate([b_high, b_high, b_low], axis=0))


def swap(a):
    return pltpu.roll(a, 64, 1)


def low_lanes(rows):
    return lax.broadcasted_iota(jnp.int32, (rows, 128), 1) < 64


def pick(low, high):
    return jnp.where(low_lanes(low.shape[0]), low, high)


def eye_twice():
    row = lax.broadcasted_iota(jnp.int32, (64, 128), 0)
    lane = lax.broadcasted_iota(jnp.int32, (64, 128), 1)
    return jnp.where(lane % 64 == row, 1.0, 0.0).astype(jnp.float32)


def invert(pairs, parts):
    lane = lax.broadcasted_iota(jnp.int32, (1, 128), 1)
    spot = lane % 64
    low8, low56 = low_lanes(8), low_lanes(56)
    row8 = lax.broadcasted_iota(jnp.int32, (8, 128), 0)
    tail = lax.broadcasted_iota(jnp.int32, (64, 128), 1) % 64 >= 56

    def spread(a, j, low):
        first, second = a[:, j : j + 1], a[:, 64 + j : 65 + j]
        return jnp.where(low, jnp.broadcast_to(first, a.shape), jnp.broadcast_to(second, a.shape))

    def eight_steps(top, rest):
        tops = [spread(top, j, low8) for j in range(8)]
        if parts:
            left = jnp.where(lane < 8, rest, pltpu.roll(rest, 72, 1))
            high = left.astype(jnp.bfloat16).astype(jnp.float32)
            low = pltpu.roll(left - high, 16, 1)
            left = jnp.where(lane < 16, high, jnp.where(lane < 32, low, pltpu.roll(high, 32, 1)))
            left = left[:, :48].astype(jnp.bfloat16)
        else:
            left = [spread(rest, j, low56) for j in range(8)]
        for k in range(8):
            hit = row8 == k
            here = spot == k
            scale = 1.0 / tops[k][k : k + 1, :]
            line = jnp.where(here, scale, top[k : k + 1, :] * scale)
            top = jnp.where(hit, line, jnp.where(here, 0.0, top) - tops[k] * line)
            for j in range(k + 1, 8):
                part = tops[j][k : k + 1, :] * scale
                tops[j] = jnp.where(hit, part, tops[j] - tops[k] * part)
        rest = jnp.where(spot < 8, 0.0, rest)
        if parts:
            lines = jnp.concatenate([jnp.where(low8, top, 0.0), jnp.where(low8, 0.0, top)], axis=0)
            high, low = split(lines)
            rest = rest - dot(left, jnp.concatenate([high, high, low], axis=0))
        else:
            for k in range(8):
                rest = rest - left[k] * top[k : k + 1, :]
        whole = jnp.concatenate([rest, top], axis=0)
        whole = jnp.where(tail, pltpu.roll(whole, 56, 1), pltpu.roll(whole, 120, 1))
        return whole[0:8], whole[8:64]

    def body(_, carry):
        return tuple(eight_steps(*one) for one in carry)

    done = lax.fori_loop(0, 8, body, tuple((pair[0:8], pair[8:64]) for pair in pairs))
    return [part for one in done for part in both(jnp.concatenate(one, axis=0))]


def eye_less(product):
    return eye_twice() - product


def both(a):
    turned = swap(a)
    return pick(a, turned), pick(turned, a)


def solve_kernel(
    len_ref, ranks_in, diag_in, v_ref, u_ref, b_ref,
    sum_ref, left_ref, right_ref,
    ranks_ref, diag_ref, uall_ref, vall, lhs, stage, pair, chip, zbuf, ubuf, bbuf, agsrc, couple, first_t, second_t, early, late, front_ref,
    loc_sem, v_s, v_r, u_s, u_r, d_s, d_r, z_s, z_r, h_s, h_r, b_s, b_r, e_s, e_r, ag_s, ag_r, ad_s, ad_r,
):
    x = lax.axis_index("node")
    row = lax.axis_index("row")
    y = lax.axis_index("col")
    own_v = pltpu.make_async_copy(v_ref, vall.at[:, y], loc_sem.at[0])
    own_u = pltpu.make_async_copy(u_ref, uall_ref.at[:, y], loc_sem.at[1])
    own_b = pltpu.make_async_copy(b_ref, lhs.at[0:COLS], loc_sem.at[2])
    small = [
        pltpu.make_async_copy(src, dst, loc_sem.at[3 + i])
        for i, (src, dst) in enumerate(((ranks_in, ranks_ref), (diag_in, diag_ref)))
    ]
    for copy in small + [own_u, own_v, own_b]:
        copy.start()
    z = row // 2
    h = row % 2
    right = (x, row, (y + 1) % 4)
    left = (x, row, (y + 3) % 4)
    ypast = (y + 3) % 4
    ynext = (y + 1) % 4
    partner = (x, z * 2 + (1 - h), y)
    block = z // 4

    def z_peer(d):
        return (x, ((z + d) % 8) * 2 + h, y)

    def core_peer(d):
        return (x, (row + d) % 16, y)

    def plane_peer(d):
        return ((x + d // 4) % 4, row, (y + d % 4) % 4)

    peers = [core_peer(d) for d in range(1, 16)] + [plane_peer(d) for d in range(1, 16)]
    barrier = pltpu.get_barrier_semaphore()
    for peer in peers:
        pl.semaphore_signal(barrier, inc=1, device_id=peer, device_id_type=MESH)
    for copy in small:
        copy.wait()
    over = 1.0 / diag_ref[...]
    weight = jnp.where(lax.broadcasted_iota(jnp.int32, (1, ROWS), 1) < len_ref[0], over, 0.0)
    own_u.wait()
    eight = lax.broadcasted_iota(jnp.int32, (8, 1), 0)
    parts = []
    for half in range(2):
        for l in range(LEVELS):
            kept = jnp.where(y * 16 + half * 8 + eight < ranks_ref[l], 1.0, 0.0)
            parts.append(uall_ref[l, y, half] * kept)
    mine = jnp.concatenate(parts, axis=0)
    mine_hi = mine.astype(jnp.bfloat16)
    lhs[COLS : COLS + 48] = mine_hi
    lhs[COLS + 48 : COLS + 96] = (mine - mine_hi.astype(jnp.float32)).astype(jnp.bfloat16)
    pl.semaphore_wait(barrier, len(peers))

    def remote(src, dst, send, recv, device):
        return pltpu.make_async_remote_copy(
            src_ref=src, dst_ref=dst, send_sem=send, recv_sem=recv, device_id=device, device_id_type=MESH
        )

    sent = []

    def go(copy):
        copy.start()
        sent.append(copy)

    def start_all(copies):
        for copy in copies:
            copy.start()

    def wait_all(whole, sem):
        pltpu.make_async_copy(whole, whole, sem).wait()

    def direct(src, dst, send, recv, l):
        return (
            remote(src.at[l], dst.at[l, y], send.at[l, 0], recv.at[l, 0], right),
            remote(src.at[l], dst.at[l, y], send.at[l, 1], recv.at[l, 1], left),
        )

    def onward(dst, send, recv, l):
        return (
            remote(dst.at[l, ypast, 0], dst.at[l, ypast, 0], send.at[l, 2], recv.at[l, 2], right),
            remote(dst.at[l, ynext, 1], dst.at[l, ynext, 1], send.at[l, 3], recv.at[l, 3], left),
        )

    v_direct = [direct(v_ref, vall, v_s, v_r, l) for l in range(LEVELS)]
    v_onward = [onward(vall, v_s, v_r, l) for l in range(LEVELS)]
    u_direct = [direct(u_ref, uall_ref, u_s, u_r, l) for l in range(LEVELS)]
    u_onward = [onward(uall_ref, u_s, u_r, l) for l in range(LEVELS)]

    def send_direct(copies, l):
        for copy in copies[l]:
            go(copy)

    def pass_on(direct_copies, onward_copies, l):
        for copy in direct_copies[l]:
            copy.wait_recv()
        for copy in onward_copies[l]:
            go(copy)

    send_direct(v_direct, 0)
    send_direct(v_direct, 1)
    own_v.wait()
    own_b.wait()

    def product(l):
        for copy in v_onward[l]:
            copy.wait_recv()
        kept = jnp.where(lax.broadcasted_iota(jnp.int32, (64, 1), 0) < ranks_ref[l], 1.0, 0.0)
        total = None
        for part in range(4):
            span = slice(512 * part, 512 * part + 512)
            scaled = vall[l, :, :, :, span].reshape(64, 512) * weight[:, span] * kept
            high = scaled.astype(jnp.bfloat16)
            low = (scaled - high.astype(jnp.float32)).astype(jnp.bfloat16)
            both = jnp.concatenate([high, low], axis=0)
            term = lax.dot_general(
                lhs[:, span], both, (((1,), (1,)), ((), ())), preferred_element_type=jnp.float32
            )
            total = term if total is None else total + term
        from_b = total[0:COLS]
        from_b = (from_b + swap(from_b)).reshape(2, 8, 24, 128)
        from_u = total[COLS : COLS + 48] + total[COLS + 48 : COLS + 96]
        from_u = (from_u + swap(from_u)).reshape(2, 1, 24, 128)
        lanes = lax.broadcasted_iota(jnp.int32, (2, 8, 24, 128), 3) < 64
        stage[l] = jnp.where(lanes, from_b, from_u)

    d_copies = [remote(stage.at[l, 1 - h], pair.at[l], d_s.at[l], d_r.at[l], partner) for l in range(LEVELS)]
    z_copies = [
        [remote(chip.at[l, (z + d) % 8], zbuf.at[l, z], z_s.at[l], z_r.at[l], z_peer(d)) for d in range(1, 8)]
        for l in range(LEVELS)
    ]
    spot = x * 4 + y
    u_copies = [
        [remote(ubuf.at[l, h, spot], ubuf.at[l, h, spot], h_s.at[l], h_r.at[l], plane_peer(d)) for d in range(1, 16)]
        for l in range(LEVELS)
    ]
    b_copies = [
        [remote(bbuf.at[l, x], bbuf.at[l, x], b_s.at[l], b_r.at[l], plane_peer(4 * d)) for d in range(1, 4)]
        for l in range(LEVELS)
    ]
    share_copies = [remote(ubuf.at[l, h], ubuf.at[l, h], e_s.at[l], e_r.at[l], partner) for l in range(LEVELS)]

    def send_z(l):
        d_copies[l].wait_recv()
        chip[l] = stage[l, h] + pair[l]
        start_all(z_copies[l])
        zbuf[l, z] = chip[l, z]

    def send_plane(l):
        wait_all(zbuf.at[l, 0:7], z_r.at[l])
        first = (zbuf[l, 0] + zbuf[l, 1]) + (zbuf[l, 2] + zbuf[l, 3])
        second = (zbuf[l, 4] + zbuf[l, 5]) + (zbuf[l, 6] + zbuf[l, 7])
        ubuf[l, h, spot] = pick(swap(first), second)
        bbuf[l, x] = pick(first, swap(second))
        start_all(u_copies[l])
        start_all(b_copies[l])

    def share(l):
        wait_all(ubuf.at[l, h, 0:15], h_r.at[l])
        wait_all(bbuf.at[l, 0:3], b_r.at[l])
        go(share_copies[l])

    def gathered(l, at):
        panels = [
            jnp.concatenate(
                [ubuf[l, half, 4 * at + col, 8 * k : 8 * k + 8] for col in range(4) for half in range(2)], axis=0
            )
            for k in range(LEVELS)
        ]
        return panels[0], jnp.concatenate([panels[1], panels[2], bbuf[l, at]], axis=0)

    pass_on(v_direct, v_onward, 0)
    send_direct(v_direct, 2)
    pass_on(v_direct, v_onward, 1)
    product(0)
    go(d_copies[0])
    send_z(0)
    pass_on(v_direct, v_onward, 2)
    product(1)
    go(d_copies[1])
    send_z(1)
    product(2)
    go(d_copies[2])
    send_z(2)
    send_plane(0)
    send_plane(1)
    send_plane(2)
    for l in range(LEVELS):
        send_direct(u_direct, l)
    share(0)
    share_copies[0].wait_recv()

    zero = [[both(part) for part in gathered(0, at)] for at in range(4)]
    minus = [eye_less(mm(panel[0], panel[1])) for panel, _ in zero]
    inverse = invert([pick(minus[0], minus[1]), pick(minus[2], minus[3])], True)
    share(1)
    t_low, t_high = [], []
    for at in range(4):
        (g_low, g_high), (q_low, q_high) = zero[at]
        t_low.append(mm(q_high - mm(q_low, g_high), inverse[at]))
        t_high.append(q_low - mm(t_low[at], g_low))
        first_t[at, 0] = t_low[at][0:128]
        first_t[at, 1] = t_high[at][0:128]
    pass_on(u_direct, u_onward, 0)
    share_copies[1].wait_recv()

    def after_zero(l, at):
        lead, raw = gathered(l, at)
        n_low, n_high = both(lead)
        return raw + swap(raw) - (mm(t_low[at], n_low) + mm(t_high[at], n_high))

    w1 = [after_zero(1, at) for at in range(4)]
    for at in range(4):
        sides = pick(w1[at // 2 * 2][128:152], w1[at // 2 * 2 + 1][128:152])
        for c, t in ((0, t_low[at]), (1, t_high[at])):
            agsrc[at, c, 0:24] = t[128:152]
            agsrc[at, c, 24:48] = sides
    early_copies = [
        remote(agsrc.at[x, ((z + d) % 8) // 4], early.at[h, z], ag_s.at[0], ag_r.at[0], z_peer(d))
        for d in range(1, 8)
    ]
    start_all(early_copies)
    early[h, z] = agsrc[x, block]
    minus = [eye_less(mm(w1[at][0:64], w1[at + 1][0:64])) for at in (0, 2)]
    inverse = invert([pick(minus[0], minus[1])], False)
    share(2)
    t1 = []
    for even in (0, 2):
        low, high = w1[even], w1[even + 1]
        one = mm(high[64:152] - mm(low[64:152], high[0:64]), inverse[even // 2])
        t1 += [one, low[64:152] - mm(one, low[0:64])]
        couple[even // 2, 0] = low[0:64]
        couple[even // 2, 1] = high[0:64]
        couple[even // 2, 2] = inverse[even // 2]
    for at in range(4):
        second_t[at] = t1[at][0:64]
    pass_on(u_direct, u_onward, 1)
    pass_on(u_direct, u_onward, 2)
    share_copies[2].wait_recv()

    w2 = [after_zero(2, at) for at in range(4)]
    p2 = [w2[at][64:152] - mm(t1[at], w2[at][0:64]) for at in range(4)]
    low, high = p2[0] + p2[1], p2[2] + p2[3]
    own = jnp.where(x < 2, low, high)
    sib = jnp.where(x < 2, high, low)
    late[h * 8 + z] = pick(own[64:88], sib[64:88])
    late_copies = [
        remote(late.at[h * 8 + z], late.at[h * 8 + z], ag_s.at[1], ag_r.at[1], core_peer(d)) for d in range(1, 16)
    ]
    start_all(late_copies)
    inverse = invert([eye_less(mm(own[0:64], sib[0:64]))], False)[0]
    wait_all(early.at[h, 0:7], ag_r.at[0])
    early_share = remote(early.at[h], early.at[h], ad_s.at[0], ad_r.at[0], partner)
    go(early_share)

    a_01 = first_t[x, block, 0:64]
    a_02 = first_t[x, block, 64:128]
    a_12 = second_t[x]
    c_1 = mm(inverse, a_12)
    c_0 = mm(inverse, a_02) - mm(c_1, a_01)
    last_01 = -pick(c_0, c_1)
    last_2 = inverse[:, :64]
    last_high, last_low = split(jnp.concatenate([last_01, last_2], axis=1))
    for l in range(LEVELS):
        for copy in u_onward[l]:
            copy.wait_recv()
    place = lax.broadcasted_iota(jnp.int32, (64, 1), 0)
    kept = jnp.concatenate([jnp.where(place < ranks_ref[l], 1.0, 0.0) for l in range(LEVELS)], axis=0)
    for part in range(4):
        span = slice(512 * part, 512 * part + 512)
        panel_high, panel_low = split(uall_ref[:, :, :, :, span].reshape(192, 512) * kept)
        last = dot(last_high, panel_high) + (dot(last_low, panel_high) + dot(last_high, panel_low))
        last_h, last_l = split(last * weight[:, span])
        right_ref[0:64, span] = last_h
        right_ref[64:128, span] = last_h
        right_ref[128:192, span] = last_l
        front_ref[0:128, span] = panel_high[0:128]
        front_ref[128:256, span] = panel_low[0:128]

    early_share.wait_recv()
    t_0 = early[:, :, 0:24].reshape(COLS, 128)
    q_even, q_odd = both(early[:, :, 24:48].reshape(COLS, 128))
    t_even = mm(q_odd - mm(q_even, couple[x // 2, 1]), couple[x // 2, 2])
    t_odd = q_even - mm(t_even, couple[x // 2, 0])
    t_1 = jnp.where(x % 2 == 0, t_even, t_odd)
    t_0 = t_0 - mm(t_1, a_01)
    front_high, front_low = split(pick(t_0, t_1))
    front_left = jnp.concatenate([front_high, front_low], axis=1)
    for part in range(4):
        span = slice(512 * part, 512 * part + 512)
        panel_high = front_ref[0:128, span]
        front = dot(front_left, jnp.concatenate([panel_high, panel_high], axis=0)) + dot(
            front_high, front_ref[128:256, span]
        )
        sum_ref[:, span] = lhs[0:COLS, span].astype(jnp.float32) * over[:, span] - front * weight[:, span]

    for copy in sent:
        copy.wait_send()
    for l in range(LEVELS):
        wait_all(chip.at[l, 0:7], z_s.at[l])
        wait_all(ubuf.at[l, h, 0:15], h_s.at[l])
        wait_all(bbuf.at[l, 0:3], b_s.at[l])
    wait_all(early.at[h, 0:7], ag_s.at[0])
    wait_all(late.at[0:15], ag_r.at[1])
    q_own, q_sib = both(late[...].reshape(COLS, 128))
    rest = q_sib - mm(q_own, sib[0:64])
    rest_high = rest.astype(jnp.bfloat16).astype(jnp.float32)
    left_ref[:, 0:128] = pick(rest_high, rest - rest_high).astype(jnp.bfloat16)
    left_ref[:, 128:192] = rest_high.astype(jnp.bfloat16)[:, :64]

    wait_all(late.at[0:15], ag_s.at[1])


def final_kernel(width, sum_ref, left_ref, right_ref, out_ref):
    span = pl.ds(pl.multiple_of(pl.program_id(0) * width, width), width)
    out_ref[...] = sum_ref[:, span] - dot(left_ref[...], right_ref[:, span])


def local(basis_u, basis_v, leaf_diag, right_side, leaf_len, ranks):
    f32 = jnp.float32
    diag = leaf_diag.reshape(1, ROWS)
    vmem = pl.BlockSpec(memory_space=pltpu.VMEM)
    dma = pltpu.SemaphoreType.DMA
    total, left, right = pl.pallas_call(
        solve_kernel,
        name="gather_and_solve",
        out_shape=(
            pltpu.VMEM((COLS, ROWS), f32),
            pltpu.VMEM((COLS, 192), jnp.bfloat16),
            pltpu.VMEM((192, ROWS), jnp.bfloat16),
        ),
        in_specs=[pl.BlockSpec(memory_space=pltpu.SMEM)] + [pl.BlockSpec(memory_space=pltpu.HBM)] * 5,
        out_specs=(vmem, vmem, vmem),
        scratch_shapes=[
            pltpu.SMEM((LEVELS,), jnp.int32),
            pltpu.VMEM((1, ROWS), f32),
            pltpu.VMEM((LEVELS, 4, 2, 8, ROWS), f32),
            pltpu.VMEM((LEVELS, 4, 2, 8, ROWS), f32),
            pltpu.VMEM((COLS + 96, ROWS), jnp.bfloat16),
            pltpu.VMEM((LEVELS, 2, 8, 24, 128), f32),
            pltpu.VMEM((LEVELS, 8, 24, 128), f32),
            pltpu.VMEM((LEVELS, 8, 24, 128), f32),
            pltpu.VMEM((LEVELS, 8, 24, 128), f32),
            pltpu.VMEM((LEVELS, 2, 16, 24, 128), f32),
            pltpu.VMEM((LEVELS, 4, 24, 128), f32),
            pltpu.VMEM((4, 2, 48, 128), f32),
            pltpu.VMEM((2, 3, 64, 128), f32),
            pltpu.VMEM((4, 2, 128, 128), f32),
            pltpu.VMEM((4, 64, 128), f32),
            pltpu.VMEM((2, 8, 48, 128), f32),
            pltpu.VMEM((16, 24, 128), f32),
            pltpu.VMEM((256, ROWS), jnp.bfloat16),
            dma((5,)),
            dma((LEVELS, 4)), dma((LEVELS, 4)),
            dma((LEVELS, 4)), dma((LEVELS, 4)),
            dma((LEVELS,)), dma((LEVELS,)),
            dma((LEVELS,)), dma((LEVELS,)),
            dma((LEVELS,)), dma((LEVELS,)),
            dma((LEVELS,)), dma((LEVELS,)),
            dma((LEVELS,)), dma((LEVELS,)),
            dma((2,)), dma((2,)),
            dma((1,)), dma((1,)),
        ],
        compiler_params=pltpu.CompilerParams(
            collective_id=0, has_side_effects=True, vmem_limit_bytes=40 * 1024 * 1024
        ),
    )(
        leaf_len,
        *[
            pltpu.with_memory_space_constraint(array, pltpu.HBM)
            for array in (
                ranks,
                diag,
                basis_v.reshape(LEVELS, 2, 8, ROWS),
                basis_u.reshape(LEVELS, 2, 8, ROWS),
                right_side,
            )
        ]
    )
    width = 1024
    return pl.pallas_call(
        functools.partial(final_kernel, width),
        name="add_last_panel",
        grid=(ROWS // width,),
        out_shape=jax.ShapeDtypeStruct((COLS, ROWS), f32),
        in_specs=[vmem, vmem, vmem],
        out_specs=pl.BlockSpec((COLS, width), lambda i: (0, i)),
        compiler_params=pltpu.CompilerParams(vmem_limit_bytes=32 * 1024 * 1024),
        cost_estimate=pl.CostEstimate(flops=2 * COLS * 192 * ROWS, bytes_accessed=7200000, transcendentals=0),
    )(total, left, right)


def solution(mesh):
    in_specs = (
        P(None, "col", ("node", "row")),
        P(None, "col", ("node", "row")),
        P(("node", "row")),
        P("col", ("node", "row")),
        P(("node", "row")),
        P(),
    )
    out_specs = P("col", ("node", "row"))
    return jax.shard_map(local, mesh=mesh, in_specs=in_specs, out_specs=out_specs, check_vma=False)
```

```python
import functools

import jax
import jax.numpy as jnp
from jax import lax
from jax.experimental import pallas as pl
from jax.experimental.pallas import tpu as pltpu
from jax.sharding import PartitionSpec as P

LEVELS = 3
ROWS = 2048
COLS = 384
MESH = pl.DeviceIdType.MESH


def split(a):
    high = a.astype(jnp.bfloat16)
    return high, (a - high.astype(jnp.float32)).astype(jnp.bfloat16)


def dot(a, b):
    return jnp.dot(a, b, preferred_element_type=jnp.float32)


def mm(a, b):
    high = a.astype(jnp.bfloat16).astype(jnp.float32)
    parts = pick(high, a - high).astype(jnp.bfloat16)
    left = jnp.concatenate([parts, high.astype(jnp.bfloat16)[:, :64]], axis=1)
    b_high, b_low = split(b)
    return dot(left, jnp.concatenate([b_high, b_high, b_low], axis=0))


def swap(a):
    return pltpu.roll(a, 64, 1)


def low_lanes(rows):
    return lax.broadcasted_iota(jnp.int32, (rows, 128), 1) < 64


def pick(low, high):
    return jnp.where(low_lanes(low.shape[0]), low, high)


def eye_twice():
    row = lax.broadcasted_iota(jnp.int32, (64, 128), 0)
    lane = lax.broadcasted_iota(jnp.int32, (64, 128), 1)
    return jnp.where(lane % 64 == row, 1.0, 0.0).astype(jnp.float32)


def invert(pairs, parts):
    lane = lax.broadcasted_iota(jnp.int32, (1, 128), 1)
    spot = lane % 64
    low8, low56 = low_lanes(8), low_lanes(56)
    row8 = lax.broadcasted_iota(jnp.int32, (8, 128), 0)
    tail = lax.broadcasted_iota(jnp.int32, (64, 128), 1) % 64 >= 56

    def spread(a, j, low):
        first, second = a[:, j : j + 1], a[:, 64 + j : 65 + j]
        return jnp.where(low, jnp.broadcast_to(first, a.shape), jnp.broadcast_to(second, a.shape))

    def eight_steps(top, rest):
        tops = [spread(top, j, low8) for j in range(8)]
        if parts:
            left = jnp.where(lane < 8, rest, pltpu.roll(rest, 72, 1))
            high = left.astype(jnp.bfloat16).astype(jnp.float32)
            low = pltpu.roll(left - high, 16, 1)
            left = jnp.where(lane < 16, high, jnp.where(lane < 32, low, pltpu.roll(high, 32, 1)))
            left = left[:, :48].astype(jnp.bfloat16)
        else:
            left = [spread(rest, j, low56) for j in range(8)]
        for k in range(8):
            hit = row8 == k
            here = spot == k
            scale = 1.0 / tops[k][k : k + 1, :]
            line = jnp.where(here, scale, top[k : k + 1, :] * scale)
            top = jnp.where(hit, line, jnp.where(here, 0.0, top) - tops[k] * line)
            for j in range(k + 1, 8):
                part = tops[j][k : k + 1, :] * scale
                tops[j] = jnp.where(hit, part, tops[j] - tops[k] * part)
        rest = jnp.where(spot < 8, 0.0, rest)
        if parts:
            lines = jnp.concatenate([jnp.where(low8, top, 0.0), jnp.where(low8, 0.0, top)], axis=0)
            high, low = split(lines)
            rest = rest - dot(left, jnp.concatenate([high, high, low], axis=0))
        else:
            for k in range(8):
                rest = rest - left[k] * top[k : k + 1, :]
        whole = jnp.concatenate([rest, top], axis=0)
        whole = jnp.where(tail, pltpu.roll(whole, 56, 1), pltpu.roll(whole, 120, 1))
        return whole[0:8], whole[8:64]

    def body(_, carry):
        return tuple(eight_steps(*one) for one in carry)

    done = lax.fori_loop(0, 8, body, tuple((pair[0:8], pair[8:64]) for pair in pairs))
    return [part for one in done for part in both(jnp.concatenate(one, axis=0))]


def eye_less(product):
    return eye_twice() - product


def both(a):
    turned = swap(a)
    return pick(a, turned), pick(turned, a)


def solve_kernel(
    len_ref, ranks_in, diag_in, v_ref, u_ref, b_ref,
    sum_ref, left_ref, right_ref,
    ranks_ref, diag_ref, uall_ref, vall, lhs, stage, pair, chip, zbuf, ubuf, bbuf, agsrc, couple, first_t, second_t, early, late, front_ref, ready,
    loc_sem, v_s, v_r, u_s, u_r, d_s, d_r, z_s, z_r, h_s, h_r, b_s, b_r, e_s, e_r, ag_s, ag_r, ad_s, ad_r,
):
    x = lax.axis_index("node")
    row = lax.axis_index("row")
    y = lax.axis_index("col")
    own_v = pltpu.make_async_copy(v_ref, vall.at[:, y], loc_sem.at[0])
    own_u = pltpu.make_async_copy(u_ref, uall_ref.at[:, y], loc_sem.at[1])
    own_b = pltpu.make_async_copy(b_ref, lhs.at[0:COLS], loc_sem.at[2])
    small = [
        pltpu.make_async_copy(src, dst, loc_sem.at[3 + i])
        for i, (src, dst) in enumerate(((ranks_in, ranks_ref), (diag_in, diag_ref)))
    ]
    for copy in small + [own_u, own_v, own_b]:
        copy.start()
    z = row // 2
    h = row % 2
    right = (x, row, (y + 1) % 4)
    left = (x, row, (y + 3) % 4)
    ypast = (y + 3) % 4
    ynext = (y + 1) % 4
    partner = (x, z * 2 + (1 - h), y)
    block = z // 4

    def z_peer(d):
        return (x, ((z + d) % 8) * 2 + h, y)

    def core_peer(d):
        return (x, (row + d) % 16, y)

    def plane_peer(d):
        return ((x + d // 4) % 4, row, (y + d % 4) % 4)

    peers = [partner, z_peer(1), z_peer(7)] + [plane_peer(d) for d in (1, 3, 4, 12)]

    def tell(i):
        for peer in peers:
            pl.semaphore_signal(ready.at[i], inc=1, device_id=peer, device_id_type=MESH)

    def hear(i):
        pl.semaphore_wait(ready.at[i], len(peers))

    barrier = pltpu.get_barrier_semaphore()
    for peer in peers:
        pl.semaphore_signal(barrier, inc=1, device_id=peer, device_id_type=MESH)
    for copy in small:
        copy.wait()
    over = 1.0 / diag_ref[...]
    weight = jnp.where(lax.broadcasted_iota(jnp.int32, (1, ROWS), 1) < len_ref[0], over, 0.0)
    own_u.wait()
    eight = lax.broadcasted_iota(jnp.int32, (8, 1), 0)
    parts = []
    for half in range(2):
        for l in range(LEVELS):
            kept = jnp.where(y * 16 + half * 8 + eight < ranks_ref[l], 1.0, 0.0)
            parts.append(uall_ref[l, y, half] * kept)
    mine = jnp.concatenate(parts, axis=0)
    mine_hi = mine.astype(jnp.bfloat16)
    lhs[COLS : COLS + 48] = mine_hi
    lhs[COLS + 48 : COLS + 96] = (mine - mine_hi.astype(jnp.float32)).astype(jnp.bfloat16)
    pl.semaphore_wait(barrier, len(peers))

    def remote(src, dst, send, recv, device):
        return pltpu.make_async_remote_copy(
            src_ref=src, dst_ref=dst, send_sem=send, recv_sem=recv, device_id=device, device_id_type=MESH
        )

    sent = []

    def go(copy):
        copy.start()
        sent.append(copy)

    def start_all(copies):
        for copy in copies:
            copy.start()

    def wait_all(whole, sem):
        pltpu.make_async_copy(whole, whole, sem).wait()

    def direct(src, dst, send, recv, l):
        return (
            remote(src.at[l], dst.at[l, y], send.at[l, 0], recv.at[l, 0], right),
            remote(src.at[l], dst.at[l, y], send.at[l, 1], recv.at[l, 1], left),
        )

    def onward(dst, send, recv, l):
        return (
            remote(dst.at[l, ypast, 0], dst.at[l, ypast, 0], send.at[l, 2], recv.at[l, 2], right),
            remote(dst.at[l, ynext, 1], dst.at[l, ynext, 1], send.at[l, 3], recv.at[l, 3], left),
        )

    v_direct = [direct(v_ref, vall, v_s, v_r, l) for l in range(LEVELS)]
    v_onward = [onward(vall, v_s, v_r, l) for l in range(LEVELS)]
    u_direct = [direct(u_ref, uall_ref, u_s, u_r, l) for l in range(LEVELS)]
    u_onward = [onward(uall_ref, u_s, u_r, l) for l in range(LEVELS)]

    def send_direct(copies, l):
        for copy in copies[l]:
            go(copy)

    def pass_on(direct_copies, onward_copies, l):
        for copy in direct_copies[l]:
            copy.wait_recv()
        for copy in onward_copies[l]:
            go(copy)

    send_direct(v_direct, 0)
    send_direct(v_direct, 1)
    tell(0)
    own_v.wait()
    own_b.wait()

    def product(l):
        for copy in v_onward[l]:
            copy.wait_recv()
        kept = jnp.where(lax.broadcasted_iota(jnp.int32, (64, 1), 0) < ranks_ref[l], 1.0, 0.0)
        total = None
        for part in range(4):
            span = slice(512 * part, 512 * part + 512)
            scaled = vall[l, :, :, :, span].reshape(64, 512) * weight[:, span] * kept
            high = scaled.astype(jnp.bfloat16)
            low = (scaled - high.astype(jnp.float32)).astype(jnp.bfloat16)
            both = jnp.concatenate([high, low], axis=0)
            term = lax.dot_general(
                lhs[:, span], both, (((1,), (1,)), ((), ())), preferred_element_type=jnp.float32
            )
            total = term if total is None else total + term
        from_b = total[0:COLS]
        from_b = (from_b + swap(from_b)).reshape(2, 8, 24, 128)
        from_u = total[COLS : COLS + 48] + total[COLS + 48 : COLS + 96]
        from_u = (from_u + swap(from_u)).reshape(2, 1, 24, 128)
        lanes = lax.broadcasted_iota(jnp.int32, (2, 8, 24, 128), 3) < 64
        stage[l] = jnp.where(lanes, from_b, from_u)

    d_copies = [remote(stage.at[l, 1 - h], pair.at[l], d_s.at[l], d_r.at[l], partner) for l in range(LEVELS)]
    z_copies = [
        [remote(chip.at[l, (z + d) % 8], zbuf.at[l, z], z_s.at[l], z_r.at[l], z_peer(d)) for d in range(1, 8)]
        for l in range(LEVELS)
    ]
    spot = x * 4 + y
    u_copies = [
        [remote(ubuf.at[l, h, spot], ubuf.at[l, h, spot], h_s.at[l], h_r.at[l], plane_peer(d)) for d in range(1, 16)]
        for l in range(LEVELS)
    ]
    b_copies = [
        [remote(bbuf.at[l, x], bbuf.at[l, x], b_s.at[l], b_r.at[l], plane_peer(4 * d)) for d in range(1, 4)]
        for l in range(LEVELS)
    ]
    share_copies = [remote(ubuf.at[l, h], ubuf.at[l, h], e_s.at[l], e_r.at[l], partner) for l in range(LEVELS)]

    def send_z(l):
        d_copies[l].wait_recv()
        chip[l] = stage[l, h] + pair[l]
        start_all(z_copies[l])
        zbuf[l, z] = chip[l, z]

    def send_plane(l):
        wait_all(zbuf.at[l, 0:7], z_r.at[l])
        first = (zbuf[l, 0] + zbuf[l, 1]) + (zbuf[l, 2] + zbuf[l, 3])
        second = (zbuf[l, 4] + zbuf[l, 5]) + (zbuf[l, 6] + zbuf[l, 7])
        ubuf[l, h, spot] = pick(swap(first), second)
        bbuf[l, x] = pick(first, swap(second))
        start_all(u_copies[l])
        start_all(b_copies[l])

    def share(l):
        wait_all(ubuf.at[l, h, 0:15], h_r.at[l])
        wait_all(bbuf.at[l, 0:3], b_r.at[l])
        go(share_copies[l])

    def gathered(l, at):
        panels = [
            jnp.concatenate(
                [ubuf[l, half, 4 * at + col, 8 * k : 8 * k + 8] for col in range(4) for half in range(2)], axis=0
            )
            for k in range(LEVELS)
        ]
        return panels[0], jnp.concatenate([panels[1], panels[2], bbuf[l, at]], axis=0)

    pass_on(v_direct, v_onward, 0)
    send_direct(v_direct, 2)
    hear(0)
    tell(1)
    pass_on(v_direct, v_onward, 1)
    hear(1)
    tell(2)
    product(0)
    go(d_copies[0])
    hear(2)
    send_z(0)
    tell(3)
    pass_on(v_direct, v_onward, 2)
    product(1)
    go(d_copies[1])
    send_z(1)
    product(2)
    go(d_copies[2])
    send_z(2)
    send_plane(0)
    send_plane(1)
    send_plane(2)
    for l in range(LEVELS):
        send_direct(u_direct, l)
    share(0)
    share_copies[0].wait_recv()

    zero = [[both(part) for part in gathered(0, at)] for at in range(4)]
    minus = [eye_less(mm(panel[0], panel[1])) for panel, _ in zero]
    inverse = invert([pick(minus[0], minus[1]), pick(minus[2], minus[3])], True)
    share(1)
    t_low, t_high = [], []
    for at in range(4):
        (g_low, g_high), (q_low, q_high) = zero[at]
        t_low.append(mm(q_high - mm(q_low, g_high), inverse[at]))
        t_high.append(q_low - mm(t_low[at], g_low))
        first_t[at, 0] = t_low[at][0:128]
        first_t[at, 1] = t_high[at][0:128]
    pass_on(u_direct, u_onward, 0)
    share_copies[1].wait_recv()

    def after_zero(l, at):
        lead, raw = gathered(l, at)
        n_low, n_high = both(lead)
        return raw + swap(raw) - (mm(t_low[at], n_low) + mm(t_high[at], n_high))

    w1 = [after_zero(1, at) for at in range(4)]
    for at in range(4):
        sides = pick(w1[at // 2 * 2][128:152], w1[at // 2 * 2 + 1][128:152])
        for c, t in ((0, t_low[at]), (1, t_high[at])):
            agsrc[at, c, 0:24] = t[128:152]
            agsrc[at, c, 24:48] = sides
    early_copies = [
        remote(agsrc.at[x, ((z + d) % 8) // 4], early.at[h, z], ag_s.at[0], ag_r.at[0], z_peer(d))
        for d in range(1, 8)
    ]
    start_all(early_copies)
    early[h, z] = agsrc[x, block]
    minus = [eye_less(mm(w1[at][0:64], w1[at + 1][0:64])) for at in (0, 2)]
    inverse = invert([pick(minus[0], minus[1])], False)
    share(2)
    t1 = []
    for even in (0, 2):
        low, high = w1[even], w1[even + 1]
        one = mm(high[64:152] - mm(low[64:152], high[0:64]), inverse[even // 2])
        t1 += [one, low[64:152] - mm(one, low[0:64])]
        couple[even // 2, 0] = low[0:64]
        couple[even // 2, 1] = high[0:64]
        couple[even // 2, 2] = inverse[even // 2]
    for at in range(4):
        second_t[at] = t1[at][0:64]
    pass_on(u_direct, u_onward, 1)
    pass_on(u_direct, u_onward, 2)
    share_copies[2].wait_recv()

    w2 = [after_zero(2, at) for at in range(4)]
    p2 = [w2[at][64:152] - mm(t1[at], w2[at][0:64]) for at in range(4)]
    low, high = p2[0] + p2[1], p2[2] + p2[3]
    own = jnp.where(x < 2, low, high)
    sib = jnp.where(x < 2, high, low)
    late[h * 8 + z] = pick(own[64:88], sib[64:88])
    late_copies = [
        remote(late.at[h * 8 + z], late.at[h * 8 + z], ag_s.at[1], ag_r.at[1], core_peer(d)) for d in range(1, 16)
    ]
    hear(3)
    start_all(late_copies)
    inverse = invert([eye_less(mm(own[0:64], sib[0:64]))], False)[0]
    wait_all(early.at[h, 0:7], ag_r.at[0])
    early_share = remote(early.at[h], early.at[h], ad_s.at[0], ad_r.at[0], partner)
    go(early_share)

    a_01 = first_t[x, block, 0:64]
    a_02 = first_t[x, block, 64:128]
    a_12 = second_t[x]
    c_1 = mm(inverse, a_12)
    c_0 = mm(inverse, a_02) - mm(c_1, a_01)
    last_01 = -pick(c_0, c_1)
    last_2 = inverse[:, :64]
    last_high, last_low = split(jnp.concatenate([last_01, last_2], axis=1))
    for l in range(LEVELS):
        for copy in u_onward[l]:
            copy.wait_recv()
    place = lax.broadcasted_iota(jnp.int32, (64, 1), 0)
    kept = jnp.concatenate([jnp.where(place < ranks_ref[l], 1.0, 0.0) for l in range(LEVELS)], axis=0)
    for part in range(4):
        span = slice(512 * part, 512 * part + 512)
        panel_high, panel_low = split(uall_ref[:, :, :, :, span].reshape(192, 512) * kept)
        last = dot(last_high, panel_high) + (dot(last_low, panel_high) + dot(last_high, panel_low))
        last_h, last_l = split(last * weight[:, span])
        right_ref[0:64, span] = last_h
        right_ref[64:128, span] = last_h
        right_ref[128:192, span] = last_l
        front_ref[0:128, span] = panel_high[0:128]
        front_ref[128:256, span] = panel_low[0:128]

    early_share.wait_recv()
    t_0 = early[:, :, 0:24].reshape(COLS, 128)
    q_even, q_odd = both(early[:, :, 24:48].reshape(COLS, 128))
    t_even = mm(q_odd - mm(q_even, couple[x // 2, 1]), couple[x // 2, 2])
    t_odd = q_even - mm(t_even, couple[x // 2, 0])
    t_1 = jnp.where(x % 2 == 0, t_even, t_odd)
    t_0 = t_0 - mm(t_1, a_01)
    front_high, front_low = split(pick(t_0, t_1))
    front_left = jnp.concatenate([front_high, front_low], axis=1)
    for part in range(4):
        span = slice(512 * part, 512 * part + 512)
        panel_high = front_ref[0:128, span]
        front = dot(front_left, jnp.concatenate([panel_high, panel_high], axis=0)) + dot(
            front_high, front_ref[128:256, span]
        )
        sum_ref[:, span] = lhs[0:COLS, span].astype(jnp.float32) * over[:, span] - front * weight[:, span]

    for copy in sent:
        copy.wait_send()
    for l in range(LEVELS):
        wait_all(chip.at[l, 0:7], z_s.at[l])
        wait_all(ubuf.at[l, h, 0:15], h_s.at[l])
        wait_all(bbuf.at[l, 0:3], b_s.at[l])
    wait_all(early.at[h, 0:7], ag_s.at[0])
    wait_all(late.at[0:15], ag_r.at[1])
    q_own, q_sib = both(late[...].reshape(COLS, 128))
    rest = q_sib - mm(q_own, sib[0:64])
    rest_high = rest.astype(jnp.bfloat16).astype(jnp.float32)
    left_ref[:, 0:128] = pick(rest_high, rest - rest_high).astype(jnp.bfloat16)
    left_ref[:, 128:192] = rest_high.astype(jnp.bfloat16)[:, :64]

    wait_all(late.at[0:15], ag_s.at[1])


def final_kernel(width, sum_ref, left_ref, right_ref, out_ref):
    span = pl.ds(pl.multiple_of(pl.program_id(0) * width, width), width)
    out_ref[...] = sum_ref[:, span] - dot(left_ref[...], right_ref[:, span])


def local(basis_u, basis_v, leaf_diag, right_side, leaf_len, ranks):
    f32 = jnp.float32
    diag = leaf_diag.reshape(1, ROWS)
    vmem = pl.BlockSpec(memory_space=pltpu.VMEM)
    dma = pltpu.SemaphoreType.DMA
    total, left, right = pl.pallas_call(
        solve_kernel,
        name="gather_and_solve",
        out_shape=(
            pltpu.VMEM((COLS, ROWS), f32),
            pltpu.VMEM((COLS, 192), jnp.bfloat16),
            pltpu.VMEM((192, ROWS), jnp.bfloat16),
        ),
        in_specs=[pl.BlockSpec(memory_space=pltpu.SMEM)] + [pl.BlockSpec(memory_space=pltpu.HBM)] * 5,
        out_specs=(vmem, vmem, vmem),
        scratch_shapes=[
            pltpu.SMEM((LEVELS,), jnp.int32),
            pltpu.VMEM((1, ROWS), f32),
            pltpu.VMEM((LEVELS, 4, 2, 8, ROWS), f32),
            pltpu.VMEM((LEVELS, 4, 2, 8, ROWS), f32),
            pltpu.VMEM((COLS + 96, ROWS), jnp.bfloat16),
            pltpu.VMEM((LEVELS, 2, 8, 24, 128), f32),
            pltpu.VMEM((LEVELS, 8, 24, 128), f32),
            pltpu.VMEM((LEVELS, 8, 24, 128), f32),
            pltpu.VMEM((LEVELS, 8, 24, 128), f32),
            pltpu.VMEM((LEVELS, 2, 16, 24, 128), f32),
            pltpu.VMEM((LEVELS, 4, 24, 128), f32),
            pltpu.VMEM((4, 2, 48, 128), f32),
            pltpu.VMEM((2, 3, 64, 128), f32),
            pltpu.VMEM((4, 2, 128, 128), f32),
            pltpu.VMEM((4, 64, 128), f32),
            pltpu.VMEM((2, 8, 48, 128), f32),
            pltpu.VMEM((16, 24, 128), f32),
            pltpu.VMEM((256, ROWS), jnp.bfloat16),
            pltpu.SemaphoreType.REGULAR((4,)),
            dma((5,)),
            dma((LEVELS, 4)), dma((LEVELS, 4)),
            dma((LEVELS, 4)), dma((LEVELS, 4)),
            dma((LEVELS,)), dma((LEVELS,)),
            dma((LEVELS,)), dma((LEVELS,)),
            dma((LEVELS,)), dma((LEVELS,)),
            dma((LEVELS,)), dma((LEVELS,)),
            dma((LEVELS,)), dma((LEVELS,)),
            dma((2,)), dma((2,)),
            dma((1,)), dma((1,)),
        ],
        compiler_params=pltpu.CompilerParams(
            collective_id=0, has_side_effects=True, vmem_limit_bytes=40 * 1024 * 1024
        ),
    )(
        leaf_len,
        *[
            pltpu.with_memory_space_constraint(array, pltpu.HBM)
            for array in (
                ranks,
                diag,
                basis_v.reshape(LEVELS, 2, 8, ROWS),
                basis_u.reshape(LEVELS, 2, 8, ROWS),
                right_side,
            )
        ]
    )
    width = 1024
    return pl.pallas_call(
        functools.partial(final_kernel, width),
        name="add_last_panel",
        grid=(ROWS // width,),
        out_shape=jax.ShapeDtypeStruct((COLS, ROWS), f32),
        in_specs=[vmem, vmem, vmem],
        out_specs=pl.BlockSpec((COLS, width), lambda i: (0, i)),
        compiler_params=pltpu.CompilerParams(vmem_limit_bytes=32 * 1024 * 1024),
        cost_estimate=pl.CostEstimate(flops=2 * COLS * 192 * ROWS, bytes_accessed=7200000, transcendentals=0),
    )(total, left, right)


def solution(mesh):
    in_specs = (
        P(None, "col", ("node", "row")),
        P(None, "col", ("node", "row")),
        P(("node", "row")),
        P("col", ("node", "row")),
        P(("node", "row")),
        P(),
    )
    out_specs = P("col", ("node", "row"))
    return jax.shard_map(local, mesh=mesh, in_specs=in_specs, out_specs=out_specs, check_vma=False)
```

```python
import functools

import jax
import jax.numpy as jnp
from jax import lax
from jax.experimental import pallas as pl
from jax.experimental.pallas import tpu as pltpu
from jax.sharding import PartitionSpec as P

LEVELS = 3
ROWS = 2048
COLS = 384
MESH = pl.DeviceIdType.MESH
FAR_Z = (4, 3, 5, 2, 6, 1, 7)
FAR_CORE = (8, 7, 9, 6, 10, 5, 11, 4, 12, 3, 13, 2, 14, 1, 15)
FAR_PLANE = (10, 6, 14, 9, 11, 2, 8, 5, 7, 13, 15, 1, 3, 4, 12)


def split(a):
    high = a.astype(jnp.bfloat16)
    return high, (a - high.astype(jnp.float32)).astype(jnp.bfloat16)


def dot(a, b):
    return jnp.dot(a, b, preferred_element_type=jnp.float32)


def mm(a, b):
    high = a.astype(jnp.bfloat16).astype(jnp.float32)
    parts = pick(high, a - high).astype(jnp.bfloat16)
    left = jnp.concatenate([parts, high.astype(jnp.bfloat16)[:, :64]], axis=1)
    b_high, b_low = split(b)
    return dot(left, jnp.concatenate([b_high, b_high, b_low], axis=0))


def swap(a):
    return pltpu.roll(a, 64, 1)


def low_lanes(rows):
    return lax.broadcasted_iota(jnp.int32, (rows, 128), 1) < 64


def pick(low, high):
    return jnp.where(low_lanes(low.shape[0]), low, high)


def eye_twice():
    row = lax.broadcasted_iota(jnp.int32, (64, 128), 0)
    lane = lax.broadcasted_iota(jnp.int32, (64, 128), 1)
    return jnp.where(lane % 64 == row, 1.0, 0.0).astype(jnp.float32)


def invert(pairs, parts):
    lane = lax.broadcasted_iota(jnp.int32, (1, 128), 1)
    spot = lane % 64
    low8, low56 = low_lanes(8), low_lanes(56)
    row8 = lax.broadcasted_iota(jnp.int32, (8, 128), 0)
    tail = lax.broadcasted_iota(jnp.int32, (64, 128), 1) % 64 >= 56

    def spread(a, j, low):
        first, second = a[:, j : j + 1], a[:, 64 + j : 65 + j]
        return jnp.where(low, jnp.broadcast_to(first, a.shape), jnp.broadcast_to(second, a.shape))

    def eight_steps(top, rest):
        tops = [spread(top, j, low8) for j in range(8)]
        if parts:
            left = jnp.where(lane < 8, rest, pltpu.roll(rest, 72, 1))
            high = left.astype(jnp.bfloat16).astype(jnp.float32)
            low = pltpu.roll(left - high, 16, 1)
            left = jnp.where(lane < 16, high, jnp.where(lane < 32, low, pltpu.roll(high, 32, 1)))
            left = left[:, :48].astype(jnp.bfloat16)
        else:
            left = [spread(rest, j, low56) for j in range(8)]
        for k in range(8):
            hit = row8 == k
            here = spot == k
            scale = 1.0 / tops[k][k : k + 1, :]
            line = jnp.where(here, scale, top[k : k + 1, :] * scale)
            top = jnp.where(hit, line, jnp.where(here, 0.0, top) - tops[k] * line)
            for j in range(k + 1, 8):
                part = tops[j][k : k + 1, :] * scale
                tops[j] = jnp.where(hit, part, tops[j] - tops[k] * part)
        rest = jnp.where(spot < 8, 0.0, rest)
        if parts:
            lines = jnp.concatenate([jnp.where(low8, top, 0.0), jnp.where(low8, 0.0, top)], axis=0)
            high, low = split(lines)
            rest = rest - dot(left, jnp.concatenate([high, high, low], axis=0))
        else:
            for k in range(8):
                rest = rest - left[k] * top[k : k + 1, :]
        whole = jnp.concatenate([rest, top], axis=0)
        whole = jnp.where(tail, pltpu.roll(whole, 56, 1), pltpu.roll(whole, 120, 1))
        return whole[0:8], whole[8:64]

    def body(_, carry):
        return tuple(eight_steps(*one) for one in carry)

    done = lax.fori_loop(0, 8, body, tuple((pair[0:8], pair[8:64]) for pair in pairs))
    return [part for one in done for part in both(jnp.concatenate(one, axis=0))]


def eye_less(product):
    return eye_twice() - product


def both(a):
    turned = swap(a)
    return pick(a, turned), pick(turned, a)


def solve_kernel(
    len_ref, ranks_in, diag_in, v_ref, u_ref, b_ref,
    sum_ref, left_ref, right_ref,
    ranks_ref, diag_ref, uall_ref, vall, lhs, stage, pair, chip, zbuf, ubuf, bbuf, agsrc, couple, first_t, second_t, early, late, front_ref, ready,
    loc_sem, v_s, v_r, u_s, u_r, d_s, d_r, z_s, z_r, h_s, h_r, b_s, b_r, e_s, e_r, ag_s, ag_r, ad_s, ad_r,
):
    x = lax.axis_index("node")
    row = lax.axis_index("row")
    y = lax.axis_index("col")
    own_v = pltpu.make_async_copy(v_ref, vall.at[:, y], loc_sem.at[0])
    own_u = pltpu.make_async_copy(u_ref, uall_ref.at[:, y], loc_sem.at[1])
    own_b = pltpu.make_async_copy(b_ref, lhs.at[0:COLS], loc_sem.at[2])
    small = [
        pltpu.make_async_copy(src, dst, loc_sem.at[3 + i])
        for i, (src, dst) in enumerate(((ranks_in, ranks_ref), (diag_in, diag_ref)))
    ]
    for copy in small + [own_u, own_v, own_b]:
        copy.start()
    z = row // 2
    h = row % 2
    right = (x, row, (y + 1) % 4)
    left = (x, row, (y + 3) % 4)
    ypast = (y + 3) % 4
    ynext = (y + 1) % 4
    partner = (x, z * 2 + (1 - h), y)
    block = z // 4

    def z_peer(d):
        return (x, ((z + d) % 8) * 2 + h, y)

    def core_peer(d):
        return (x, (row + d) % 16, y)

    def plane_peer(d):
        return ((x + d // 4) % 4, row, (y + d % 4) % 4)

    peers = [partner, z_peer(1), z_peer(7)] + [plane_peer(d) for d in (1, 3, 4, 12)]

    def tell(i):
        for peer in peers:
            pl.semaphore_signal(ready.at[i], inc=1, device_id=peer, device_id_type=MESH)

    def hear(i):
        pl.semaphore_wait(ready.at[i], len(peers))

    barrier = pltpu.get_barrier_semaphore()
    for peer in peers:
        pl.semaphore_signal(barrier, inc=1, device_id=peer, device_id_type=MESH)
    for copy in small:
        copy.wait()
    over = 1.0 / diag_ref[...]
    weight = jnp.where(lax.broadcasted_iota(jnp.int32, (1, ROWS), 1) < len_ref[0], over, 0.0)
    own_u.wait()
    eight = lax.broadcasted_iota(jnp.int32, (8, 1), 0)
    parts = []
    for half in range(2):
        for l in range(LEVELS):
            kept = jnp.where(y * 16 + half * 8 + eight < ranks_ref[l], 1.0, 0.0)
            parts.append(uall_ref[l, y, half] * kept)
    mine = jnp.concatenate(parts, axis=0)
    mine_hi = mine.astype(jnp.bfloat16)
    lhs[COLS : COLS + 48] = mine_hi
    lhs[COLS + 48 : COLS + 96] = (mine - mine_hi.astype(jnp.float32)).astype(jnp.bfloat16)
    pl.semaphore_wait(barrier, len(peers))

    def remote(src, dst, send, recv, device):
        return pltpu.make_async_remote_copy(
            src_ref=src, dst_ref=dst, send_sem=send, recv_sem=recv, device_id=device, device_id_type=MESH
        )

    sent = []

    def go(copy):
        copy.start()
        sent.append(copy)

    def start_all(copies):
        for copy in copies:
            copy.start()

    def wait_all(whole, sem):
        pltpu.make_async_copy(whole, whole, sem).wait()

    def direct(src, dst, send, recv, l):
        return (
            remote(src.at[l], dst.at[l, y], send.at[l, 0], recv.at[l, 0], right),
            remote(src.at[l], dst.at[l, y], send.at[l, 1], recv.at[l, 1], left),
        )

    def onward(dst, send, recv, l):
        return (
            remote(dst.at[l, ypast, 0], dst.at[l, ypast, 0], send.at[l, 2], recv.at[l, 2], right),
            remote(dst.at[l, ynext, 1], dst.at[l, ynext, 1], send.at[l, 3], recv.at[l, 3], left),
        )

    v_direct = [direct(v_ref, vall, v_s, v_r, l) for l in range(LEVELS)]
    v_onward = [onward(vall, v_s, v_r, l) for l in range(LEVELS)]
    u_direct = [direct(u_ref, uall_ref, u_s, u_r, l) for l in range(LEVELS)]
    u_onward = [onward(uall_ref, u_s, u_r, l) for l in range(LEVELS)]

    def send_direct(copies, l):
        for copy in copies[l]:
            go(copy)

    def pass_on(direct_copies, onward_copies, l):
        for copy in direct_copies[l]:
            copy.wait_recv()
        for copy in onward_copies[l]:
            go(copy)

    send_direct(v_direct, 0)
    send_direct(v_direct, 1)
    tell(0)
    own_v.wait()
    own_b.wait()

    def product(l):
        for copy in v_onward[l]:
            copy.wait_recv()
        kept = jnp.where(lax.broadcasted_iota(jnp.int32, (64, 1), 0) < ranks_ref[l], 1.0, 0.0)
        total = None
        for part in range(4):
            span = slice(512 * part, 512 * part + 512)
            scaled = vall[l, :, :, :, span].reshape(64, 512) * weight[:, span] * kept
            high = scaled.astype(jnp.bfloat16)
            low = (scaled - high.astype(jnp.float32)).astype(jnp.bfloat16)
            both = jnp.concatenate([high, low], axis=0)
            term = lax.dot_general(
                lhs[:, span], both, (((1,), (1,)), ((), ())), preferred_element_type=jnp.float32
            )
            total = term if total is None else total + term
        from_b = total[0:COLS]
        from_b = (from_b + swap(from_b)).reshape(2, 8, 24, 128)
        from_u = total[COLS : COLS + 48] + total[COLS + 48 : COLS + 96]
        from_u = (from_u + swap(from_u)).reshape(2, 1, 24, 128)
        lanes = lax.broadcasted_iota(jnp.int32, (2, 8, 24, 128), 3) < 64
        stage[l] = jnp.where(lanes, from_b, from_u)

    d_copies = [remote(stage.at[l, 1 - h], pair.at[l], d_s.at[l], d_r.at[l], partner) for l in range(LEVELS)]
    z_copies = [
        [remote(chip.at[l, (z + d) % 8], zbuf.at[l, z], z_s.at[l], z_r.at[l], z_peer(d)) for d in FAR_Z]
        for l in range(LEVELS)
    ]
    spot = x * 4 + y
    u_copies = [
        [remote(ubuf.at[l, h, spot], ubuf.at[l, h, spot], h_s.at[l], h_r.at[l], plane_peer(d)) for d in FAR_PLANE]
        for l in range(LEVELS)
    ]
    b_copies = [
        [remote(bbuf.at[l, x], bbuf.at[l, x], b_s.at[l], b_r.at[l], plane_peer(4 * d)) for d in range(1, 4)]
        for l in range(LEVELS)
    ]
    share_copies = [remote(ubuf.at[l, h], ubuf.at[l, h], e_s.at[l], e_r.at[l], partner) for l in range(LEVELS)]

    def send_z(l):
        d_copies[l].wait_recv()
        chip[l] = stage[l, h] + pair[l]
        start_all(z_copies[l])
        zbuf[l, z] = chip[l, z]

    def send_plane(l):
        wait_all(zbuf.at[l, 0:7], z_r.at[l])
        first = (zbuf[l, 0] + zbuf[l, 1]) + (zbuf[l, 2] + zbuf[l, 3])
        second = (zbuf[l, 4] + zbuf[l, 5]) + (zbuf[l, 6] + zbuf[l, 7])
        ubuf[l, h, spot] = pick(swap(first), second)
        bbuf[l, x] = pick(first, swap(second))
        start_all(u_copies[l])
        start_all(b_copies[l])

    def share(l):
        wait_all(ubuf.at[l, h, 0:15], h_r.at[l])
        wait_all(bbuf.at[l, 0:3], b_r.at[l])
        go(share_copies[l])

    def gathered(l, at):
        panels = [
            jnp.concatenate(
                [ubuf[l, half, 4 * at + col, 8 * k : 8 * k + 8] for col in range(4) for half in range(2)], axis=0
            )
            for k in range(LEVELS)
        ]
        return panels[0], jnp.concatenate([panels[1], panels[2], bbuf[l, at]], axis=0)

    pass_on(v_direct, v_onward, 0)
    send_direct(v_direct, 2)
    hear(0)
    tell(1)
    pass_on(v_direct, v_onward, 1)
    hear(1)
    tell(2)
    product(0)
    go(d_copies[0])
    hear(2)
    send_z(0)
    tell(3)
    pass_on(v_direct, v_onward, 2)
    product(1)
    go(d_copies[1])
    send_z(1)
    product(2)
    go(d_copies[2])
    send_z(2)
    send_plane(0)
    send_plane(1)
    send_plane(2)
    share(0)
    for l in range(LEVELS):
        send_direct(u_direct, l)
    share_copies[0].wait_recv()

    zero = [[both(part) for part in gathered(0, at)] for at in range(4)]
    minus = [eye_less(mm(panel[0], panel[1])) for panel, _ in zero]
    inverse = invert([pick(minus[0], minus[1]), pick(minus[2], minus[3])], True)
    share(1)
    t_low, t_high = [], []
    for at in range(4):
        (g_low, g_high), (q_low, q_high) = zero[at]
        t_low.append(mm(q_high - mm(q_low, g_high), inverse[at]))
        t_high.append(q_low - mm(t_low[at], g_low))
        first_t[at, 0] = t_low[at][0:128]
        first_t[at, 1] = t_high[at][0:128]
    pass_on(u_direct, u_onward, 0)
    share_copies[1].wait_recv()

    def after_zero(l, at):
        lead, raw = gathered(l, at)
        n_low, n_high = both(lead)
        return raw + swap(raw) - (mm(t_low[at], n_low) + mm(t_high[at], n_high))

    w1 = [after_zero(1, at) for at in range(4)]
    for at in range(4):
        sides = pick(w1[at // 2 * 2][128:152], w1[at // 2 * 2 + 1][128:152])
        for c, t in ((0, t_low[at]), (1, t_high[at])):
            agsrc[at, c, 0:24] = t[128:152]
            agsrc[at, c, 24:48] = sides
    early_copies = [
        remote(agsrc.at[x, ((z + d) % 8) // 4], early.at[h, z], ag_s.at[0], ag_r.at[0], z_peer(d))
        for d in FAR_Z
    ]
    start_all(early_copies)
    early[h, z] = agsrc[x, block]
    minus = [eye_less(mm(w1[at][0:64], w1[at + 1][0:64])) for at in (0, 2)]
    inverse = invert([pick(minus[0], minus[1])], False)
    share(2)
    t1 = []
    for even in (0, 2):
        low, high = w1[even], w1[even + 1]
        one = mm(high[64:152] - mm(low[64:152], high[0:64]), inverse[even // 2])
        t1 += [one, low[64:152] - mm(one, low[0:64])]
        couple[even // 2, 0] = low[0:64]
        couple[even // 2, 1] = high[0:64]
        couple[even // 2, 2] = inverse[even // 2]
    for at in range(4):
        second_t[at] = t1[at][0:64]
    pass_on(u_direct, u_onward, 1)
    pass_on(u_direct, u_onward, 2)
    share_copies[2].wait_recv()

    w2 = [after_zero(2, at) for at in range(4)]
    p2 = [w2[at][64:152] - mm(t1[at], w2[at][0:64]) for at in range(4)]
    low, high = p2[0] + p2[1], p2[2] + p2[3]
    own = jnp.where(x < 2, low, high)
    sib = jnp.where(x < 2, high, low)
    late[h * 8 + z] = pick(own[64:88], sib[64:88])
    late_copies = [
        remote(late.at[h * 8 + z], late.at[h * 8 + z], ag_s.at[1], ag_r.at[1], core_peer(d)) for d in FAR_CORE
    ]
    hear(3)
    start_all(late_copies)
    inverse = invert([eye_less(mm(own[0:64], sib[0:64]))], False)[0]
    wait_all(early.at[h, 0:7], ag_r.at[0])
    early_share = remote(early.at[h], early.at[h], ad_s.at[0], ad_r.at[0], partner)
    go(early_share)

    a_01 = first_t[x, block, 0:64]
    a_02 = first_t[x, block, 64:128]
    a_12 = second_t[x]
    c_1 = mm(inverse, a_12)
    c_0 = mm(inverse, a_02) - mm(c_1, a_01)
    last_01 = -pick(c_0, c_1)
    last_2 = inverse[:, :64]
    last_high, last_low = split(jnp.concatenate([last_01, last_2], axis=1))
    for l in range(LEVELS):
        for copy in u_onward[l]:
            copy.wait_recv()
    place = lax.broadcasted_iota(jnp.int32, (64, 1), 0)
    kept = jnp.concatenate([jnp.where(place < ranks_ref[l], 1.0, 0.0) for l in range(LEVELS)], axis=0)
    for part in range(4):
        span = slice(512 * part, 512 * part + 512)
        panel_high, panel_low = split(uall_ref[:, :, :, :, span].reshape(192, 512) * kept)
        last = dot(last_high, panel_high) + (dot(last_low, panel_high) + dot(last_high, panel_low))
        last_h, last_l = split(last * weight[:, span])
        right_ref[0:64, span] = last_h
        right_ref[64:128, span] = last_h
        right_ref[128:192, span] = last_l
        front_ref[0:128, span] = panel_high[0:128]
        front_ref[128:256, span] = panel_low[0:128]

    early_share.wait_recv()
    t_0 = early[:, :, 0:24].reshape(COLS, 128)
    q_even, q_odd = both(early[:, :, 24:48].reshape(COLS, 128))
    t_even = mm(q_odd - mm(q_even, couple[x // 2, 1]), couple[x // 2, 2])
    t_odd = q_even - mm(t_even, couple[x // 2, 0])
    t_1 = jnp.where(x % 2 == 0, t_even, t_odd)
    t_0 = t_0 - mm(t_1, a_01)
    front_high, front_low = split(pick(t_0, t_1))
    front_left = jnp.concatenate([front_high, front_low], axis=1)
    for part in range(4):
        span = slice(512 * part, 512 * part + 512)
        panel_high = front_ref[0:128, span]
        front = dot(front_left, jnp.concatenate([panel_high, panel_high], axis=0)) + dot(
            front_high, front_ref[128:256, span]
        )
        sum_ref[:, span] = lhs[0:COLS, span].astype(jnp.float32) * over[:, span] - front * weight[:, span]

    for copy in sent:
        copy.wait_send()
    for l in range(LEVELS):
        wait_all(chip.at[l, 0:7], z_s.at[l])
        wait_all(ubuf.at[l, h, 0:15], h_s.at[l])
        wait_all(bbuf.at[l, 0:3], b_s.at[l])
    wait_all(early.at[h, 0:7], ag_s.at[0])
    wait_all(late.at[0:15], ag_r.at[1])
    q_own, q_sib = both(late[...].reshape(COLS, 128))
    rest = q_sib - mm(q_own, sib[0:64])
    rest_high = rest.astype(jnp.bfloat16).astype(jnp.float32)
    left_ref[:, 0:128] = pick(rest_high, rest - rest_high).astype(jnp.bfloat16)
    left_ref[:, 128:192] = rest_high.astype(jnp.bfloat16)[:, :64]

    wait_all(late.at[0:15], ag_s.at[1])


def final_kernel(width, sum_ref, left_ref, right_ref, out_ref):
    span = pl.ds(pl.multiple_of(pl.program_id(0) * width, width), width)
    out_ref[...] = sum_ref[:, span] - dot(left_ref[...], right_ref[:, span])


def local(basis_u, basis_v, leaf_diag, right_side, leaf_len, ranks):
    f32 = jnp.float32
    diag = leaf_diag.reshape(1, ROWS)
    vmem = pl.BlockSpec(memory_space=pltpu.VMEM)
    dma = pltpu.SemaphoreType.DMA
    total, left, right = pl.pallas_call(
        solve_kernel,
        name="gather_and_solve",
        out_shape=(
            pltpu.VMEM((COLS, ROWS), f32),
            pltpu.VMEM((COLS, 192), jnp.bfloat16),
            pltpu.VMEM((192, ROWS), jnp.bfloat16),
        ),
        in_specs=[pl.BlockSpec(memory_space=pltpu.SMEM)] + [pl.BlockSpec(memory_space=pltpu.HBM)] * 5,
        out_specs=(vmem, vmem, vmem),
        scratch_shapes=[
            pltpu.SMEM((LEVELS,), jnp.int32),
            pltpu.VMEM((1, ROWS), f32),
            pltpu.VMEM((LEVELS, 4, 2, 8, ROWS), f32),
            pltpu.VMEM((LEVELS, 4, 2, 8, ROWS), f32),
            pltpu.VMEM((COLS + 96, ROWS), jnp.bfloat16),
            pltpu.VMEM((LEVELS, 2, 8, 24, 128), f32),
            pltpu.VMEM((LEVELS, 8, 24, 128), f32),
            pltpu.VMEM((LEVELS, 8, 24, 128), f32),
            pltpu.VMEM((LEVELS, 8, 24, 128), f32),
            pltpu.VMEM((LEVELS, 2, 16, 24, 128), f32),
            pltpu.VMEM((LEVELS, 4, 24, 128), f32),
            pltpu.VMEM((4, 2, 48, 128), f32),
            pltpu.VMEM((2, 3, 64, 128), f32),
            pltpu.VMEM((4, 2, 128, 128), f32),
            pltpu.VMEM((4, 64, 128), f32),
            pltpu.VMEM((2, 8, 48, 128), f32),
            pltpu.VMEM((16, 24, 128), f32),
            pltpu.VMEM((256, ROWS), jnp.bfloat16),
            pltpu.SemaphoreType.REGULAR((4,)),
            dma((5,)),
            dma((LEVELS, 4)), dma((LEVELS, 4)),
            dma((LEVELS, 4)), dma((LEVELS, 4)),
            dma((LEVELS,)), dma((LEVELS,)),
            dma((LEVELS,)), dma((LEVELS,)),
            dma((LEVELS,)), dma((LEVELS,)),
            dma((LEVELS,)), dma((LEVELS,)),
            dma((LEVELS,)), dma((LEVELS,)),
            dma((2,)), dma((2,)),
            dma((1,)), dma((1,)),
        ],
        compiler_params=pltpu.CompilerParams(
            collective_id=0, has_side_effects=True, vmem_limit_bytes=40 * 1024 * 1024
        ),
    )(
        leaf_len,
        *[
            pltpu.with_memory_space_constraint(array, pltpu.HBM)
            for array in (
                ranks,
                diag,
                basis_v.reshape(LEVELS, 2, 8, ROWS),
                basis_u.reshape(LEVELS, 2, 8, ROWS),
                right_side,
            )
        ]
    )
    width = 1024
    return pl.pallas_call(
        functools.partial(final_kernel, width),
        name="add_last_panel",
        grid=(ROWS // width,),
        out_shape=jax.ShapeDtypeStruct((COLS, ROWS), f32),
        in_specs=[vmem, vmem, vmem],
        out_specs=pl.BlockSpec((COLS, width), lambda i: (0, i)),
        compiler_params=pltpu.CompilerParams(vmem_limit_bytes=32 * 1024 * 1024),
        cost_estimate=pl.CostEstimate(flops=2 * COLS * 192 * ROWS, bytes_accessed=7200000, transcendentals=0),
    )(total, left, right)


def solution(mesh):
    in_specs = (
        P(None, "col", ("node", "row")),
        P(None, "col", ("node", "row")),
        P(("node", "row")),
        P("col", ("node", "row")),
        P(("node", "row")),
        P(),
    )
    out_specs = P("col", ("node", "row"))
    return jax.shard_map(local, mesh=mesh, in_specs=in_specs, out_specs=out_specs, check_vma=False)
```

```python
import functools

import jax
import jax.numpy as jnp
from jax import lax
from jax.experimental import pallas as pl
from jax.experimental.pallas import tpu as pltpu
from jax.sharding import PartitionSpec as P

LEVELS = 3
ROWS = 2048
COLS = 384
MESH = pl.DeviceIdType.MESH
FAR_Z = (4, 3, 5, 2, 6, 1, 7)
FAR_CORE = (8, 7, 9, 6, 10, 5, 11, 4, 12, 3, 13, 2, 14, 1, 15)
FAR_PLANE = (10, 6, 14, 9, 11, 2, 8, 5, 7, 13, 15, 1, 3, 4, 12)


def split(a):
    high = a.astype(jnp.bfloat16)
    return high, (a - high.astype(jnp.float32)).astype(jnp.bfloat16)


def dot(a, b):
    return jnp.dot(a, b, preferred_element_type=jnp.float32)


def mm(a, b):
    high = a.astype(jnp.bfloat16).astype(jnp.float32)
    parts = pick(high, a - high).astype(jnp.bfloat16)
    left = jnp.concatenate([parts, high.astype(jnp.bfloat16)[:, :64]], axis=1)
    b_high, b_low = split(b)
    return dot(left, jnp.concatenate([b_high, b_high, b_low], axis=0))


def swap(a):
    return pltpu.roll(a, 64, 1)


def low_lanes(rows):
    return lax.broadcasted_iota(jnp.int32, (rows, 128), 1) < 64


def pick(low, high):
    return jnp.where(low_lanes(low.shape[0]), low, high)


def eye_twice():
    row = lax.broadcasted_iota(jnp.int32, (64, 128), 0)
    lane = lax.broadcasted_iota(jnp.int32, (64, 128), 1)
    return jnp.where(lane % 64 == row, 1.0, 0.0).astype(jnp.float32)


def invert(pairs, parts):
    lane = lax.broadcasted_iota(jnp.int32, (1, 128), 1)
    spot = lane % 64
    low8, low56 = low_lanes(8), low_lanes(56)
    row8 = lax.broadcasted_iota(jnp.int32, (8, 128), 0)
    tail = lax.broadcasted_iota(jnp.int32, (64, 128), 1) % 64 >= 56

    def spread(a, j, low):
        first, second = a[:, j : j + 1], a[:, 64 + j : 65 + j]
        return jnp.where(low, jnp.broadcast_to(first, a.shape), jnp.broadcast_to(second, a.shape))

    def eight_steps(top, rest):
        tops = [spread(top, j, low8) for j in range(8)]
        if parts:
            left = jnp.where(lane < 8, rest, pltpu.roll(rest, 72, 1))
            high = left.astype(jnp.bfloat16).astype(jnp.float32)
            low = pltpu.roll(left - high, 16, 1)
            left = jnp.where(lane < 16, high, jnp.where(lane < 32, low, pltpu.roll(high, 32, 1)))
            left = left[:, :48].astype(jnp.bfloat16)
        else:
            left = [spread(rest, j, low56) for j in range(8)]
        for k in range(8):
            hit = row8 == k
            here = spot == k
            scale = 1.0 / tops[k][k : k + 1, :]
            line = jnp.where(here, scale, top[k : k + 1, :] * scale)
            top = jnp.where(hit, line, jnp.where(here, 0.0, top) - tops[k] * line)
            for j in range(k + 1, 8):
                part = tops[j][k : k + 1, :] * scale
                tops[j] = jnp.where(hit, part, tops[j] - tops[k] * part)
        rest = jnp.where(spot < 8, 0.0, rest)
        if parts:
            lines = jnp.concatenate([jnp.where(low8, top, 0.0), jnp.where(low8, 0.0, top)], axis=0)
            high, low = split(lines)
            rest = rest - dot(left, jnp.concatenate([high, high, low], axis=0))
        else:
            for k in range(8):
                rest = rest - left[k] * top[k : k + 1, :]
        whole = jnp.concatenate([rest, top], axis=0)
        whole = jnp.where(tail, pltpu.roll(whole, 56, 1), pltpu.roll(whole, 120, 1))
        return whole[0:8], whole[8:64]

    def body(_, carry):
        return tuple(eight_steps(*one) for one in carry)

    done = lax.fori_loop(0, 8, body, tuple((pair[0:8], pair[8:64]) for pair in pairs))
    return [part for one in done for part in both(jnp.concatenate(one, axis=0))]


def eye_less(product):
    return eye_twice() - product


def both(a):
    turned = swap(a)
    return pick(a, turned), pick(turned, a)


def solve_kernel(
    len_ref, ranks_in, diag_in, v_ref, u_ref, b_ref,
    sum_ref, left_ref, right_ref,
    ranks_ref, diag_ref, uall_ref, vall, lhs, stage, pair, chip, zbuf, ubuf, bbuf, agsrc, couple, first_t, second_t, early, late, front_ref, ready,
    loc_sem, v_s, v_r, u_s, u_r, d_s, d_r, z_s, z_r, h_s, h_r, b_s, b_r, e_s, e_r, ag_s, ag_r, ad_s, ad_r,
):
    x = lax.axis_index("node")
    row = lax.axis_index("row")
    y = lax.axis_index("col")
    own_v = pltpu.make_async_copy(v_ref, vall.at[:, y], loc_sem.at[0])
    own_u = pltpu.make_async_copy(u_ref, uall_ref.at[:, y], loc_sem.at[1])
    own_b = pltpu.make_async_copy(b_ref, lhs.at[0:COLS], loc_sem.at[2])
    small = [
        pltpu.make_async_copy(src, dst, loc_sem.at[3 + i])
        for i, (src, dst) in enumerate(((ranks_in, ranks_ref), (diag_in, diag_ref)))
    ]
    for copy in small + [own_u, own_v, own_b]:
        copy.start()
    z = row // 2
    h = row % 2
    right = (x, row, (y + 1) % 4)
    left = (x, row, (y + 3) % 4)
    ypast = (y + 3) % 4
    ynext = (y + 1) % 4
    partner = (x, z * 2 + (1 - h), y)
    block = z // 4

    def z_peer(d):
        return (x, ((z + d) % 8) * 2 + h, y)

    def core_peer(d):
        return (x, (row + d) % 16, y)

    def plane_peer(d):
        return ((x + d // 4) % 4, row, (y + d % 4) % 4)

    peers = [partner, z_peer(1), z_peer(7)] + [plane_peer(d) for d in (1, 3, 4, 12)]

    def tell(i):
        for peer in peers:
            pl.semaphore_signal(ready.at[i], inc=1, device_id=peer, device_id_type=MESH)

    def hear(i):
        pl.semaphore_wait(ready.at[i], len(peers))

    barrier = pltpu.get_barrier_semaphore()
    for peer in peers:
        pl.semaphore_signal(barrier, inc=1, device_id=peer, device_id_type=MESH)
    for copy in small:
        copy.wait()
    over = 1.0 / diag_ref[...]
    weight = jnp.where(lax.broadcasted_iota(jnp.int32, (1, ROWS), 1) < len_ref[0], over, 0.0)
    own_u.wait()
    eight = lax.broadcasted_iota(jnp.int32, (8, 1), 0)
    parts = []
    for half in range(2):
        for l in range(LEVELS):
            kept = jnp.where(y * 16 + half * 8 + eight < ranks_ref[l], 1.0, 0.0)
            parts.append(uall_ref[l, y, half] * kept)
    mine = jnp.concatenate(parts, axis=0)
    mine_hi = mine.astype(jnp.bfloat16)
    lhs[COLS : COLS + 48] = mine_hi
    lhs[COLS + 48 : COLS + 96] = (mine - mine_hi.astype(jnp.float32)).astype(jnp.bfloat16)
    pl.semaphore_wait(barrier, len(peers))

    def remote(src, dst, send, recv, device):
        return pltpu.make_async_remote_copy(
            src_ref=src, dst_ref=dst, send_sem=send, recv_sem=recv, device_id=device, device_id_type=MESH
        )

    sent = []

    def go(copy):
        copy.start()
        sent.append(copy)

    def start_all(copies):
        for copy in copies:
            copy.start()

    def wait_all(whole, sem):
        pltpu.make_async_copy(whole, whole, sem).wait()

    def direct(src, dst, send, recv, l):
        return (
            remote(src.at[l], dst.at[l, y], send.at[l, 0], recv.at[l, 0], right),
            remote(src.at[l], dst.at[l, y], send.at[l, 1], recv.at[l, 1], left),
        )

    def onward(dst, send, recv, l):
        return (
            remote(dst.at[l, ypast, 0], dst.at[l, ypast, 0], send.at[l, 2], recv.at[l, 2], right),
            remote(dst.at[l, ynext, 1], dst.at[l, ynext, 1], send.at[l, 3], recv.at[l, 3], left),
        )

    v_direct = [direct(v_ref, vall, v_s, v_r, l) for l in range(LEVELS)]
    v_onward = [onward(vall, v_s, v_r, l) for l in range(LEVELS)]
    u_direct = [direct(u_ref, uall_ref, u_s, u_r, l) for l in range(LEVELS)]
    u_onward = [onward(uall_ref, u_s, u_r, l) for l in range(LEVELS)]

    def send_direct(copies, l):
        for copy in copies[l]:
            go(copy)

    def pass_on(direct_copies, onward_copies, l):
        for copy in direct_copies[l]:
            copy.wait_recv()
        for copy in onward_copies[l]:
            go(copy)

    send_direct(v_direct, 0)
    send_direct(v_direct, 1)
    tell(0)
    own_v.wait()
    own_b.wait()

    def product(l):
        for copy in v_onward[l]:
            copy.wait_recv()
        kept = jnp.where(lax.broadcasted_iota(jnp.int32, (64, 1), 0) < ranks_ref[l], 1.0, 0.0)
        total = None
        for part in range(4):
            span = slice(512 * part, 512 * part + 512)
            scaled = vall[l, :, :, :, span].reshape(64, 512) * weight[:, span] * kept
            high = scaled.astype(jnp.bfloat16)
            low = (scaled - high.astype(jnp.float32)).astype(jnp.bfloat16)
            both = jnp.concatenate([high, low], axis=0)
            term = lax.dot_general(
                lhs[:, span], both, (((1,), (1,)), ((), ())), preferred_element_type=jnp.float32
            )
            total = term if total is None else total + term
        from_b = total[0:COLS]
        from_b = (from_b + swap(from_b)).reshape(2, 8, 24, 128)
        from_u = total[COLS : COLS + 48] + total[COLS + 48 : COLS + 96]
        from_u = (from_u + swap(from_u)).reshape(2, 1, 24, 128)
        lanes = lax.broadcasted_iota(jnp.int32, (2, 8, 24, 128), 3) < 64
        stage[l] = jnp.where(lanes, from_b, from_u)

    d_copies = [remote(stage.at[l, 1 - h], pair.at[l], d_s.at[l], d_r.at[l], partner) for l in range(LEVELS)]
    z_copies = [
        [remote(chip.at[l, (z + d) % 8], zbuf.at[l, z], z_s.at[l], z_r.at[l], z_peer(d)) for d in FAR_Z]
        for l in range(LEVELS)
    ]
    spot = x * 4 + y
    u_copies = [
        [remote(ubuf.at[l, h, spot], ubuf.at[l, h, spot], h_s.at[l], h_r.at[l], plane_peer(d)) for d in FAR_PLANE]
        for l in range(LEVELS)
    ]
    b_copies = [
        [remote(bbuf.at[l, x], bbuf.at[l, x], b_s.at[l], b_r.at[l], plane_peer(4 * d)) for d in range(1, 4)]
        for l in range(LEVELS)
    ]
    share_copies = [remote(ubuf.at[l, h], ubuf.at[l, h], e_s.at[l], e_r.at[l], partner) for l in range(LEVELS)]

    def send_z(l):
        d_copies[l].wait_recv()
        chip[l] = stage[l, h] + pair[l]
        start_all(z_copies[l])
        zbuf[l, z] = chip[l, z]

    def send_plane(l):
        wait_all(zbuf.at[l, 0:7], z_r.at[l])
        first = (zbuf[l, 0] + zbuf[l, 1]) + (zbuf[l, 2] + zbuf[l, 3])
        second = (zbuf[l, 4] + zbuf[l, 5]) + (zbuf[l, 6] + zbuf[l, 7])
        ubuf[l, h, spot] = pick(swap(first), second)
        bbuf[l, x] = pick(first, swap(second))
        start_all(u_copies[l])
        start_all(b_copies[l])

    def share(l):
        wait_all(ubuf.at[l, h, 0:15], h_r.at[l])
        wait_all(bbuf.at[l, 0:3], b_r.at[l])
        go(share_copies[l])

    def gathered(l, at):
        panels = [
            jnp.concatenate(
                [ubuf[l, half, 4 * at + col, 8 * k : 8 * k + 8] for col in range(4) for half in range(2)], axis=0
            )
            for k in range(LEVELS)
        ]
        return panels[0], jnp.concatenate([panels[1], panels[2], bbuf[l, at]], axis=0)

    pass_on(v_direct, v_onward, 0)
    send_direct(v_direct, 2)
    hear(0)
    tell(1)
    pass_on(v_direct, v_onward, 1)
    hear(1)
    tell(2)
    product(0)
    go(d_copies[0])
    hear(2)
    send_z(0)
    tell(3)
    pass_on(v_direct, v_onward, 2)
    product(1)
    go(d_copies[1])
    send_z(1)
    product(2)
    go(d_copies[2])
    send_z(2)
    send_plane(0)
    send_plane(1)
    send_plane(2)
    share(0)
    for l in range(LEVELS):
        send_direct(u_direct, l)
    share_copies[0].wait_recv()

    zero = [[both(part) for part in gathered(0, at)] for at in range(4)]
    minus = [eye_less(mm(panel[0], panel[1])) for panel, _ in zero]
    inverse = invert([pick(minus[0], minus[1]), pick(minus[2], minus[3])], True)
    share(1)
    t_low, t_high = [], []
    for at in range(4):
        (g_low, g_high), (q_low, q_high) = zero[at]
        t_low.append(mm(q_high - mm(q_low, g_high), inverse[at]))
        t_high.append(q_low - mm(t_low[at], g_low))
        first_t[at, 0] = t_low[at][0:128]
        first_t[at, 1] = t_high[at][0:128]
    pass_on(u_direct, u_onward, 0)
    share_copies[1].wait_recv()

    def after_zero(l, at):
        lead, raw = gathered(l, at)
        n_low, n_high = both(lead)
        return raw + swap(raw) - (mm(t_low[at], n_low) + mm(t_high[at], n_high))

    w1 = [after_zero(1, at) for at in range(4)]
    for at in range(4):
        sides = pick(w1[at // 2 * 2][128:152], w1[at // 2 * 2 + 1][128:152])
        for c, t in ((0, t_low[at]), (1, t_high[at])):
            agsrc[at, c, 0:24] = t[128:152]
            agsrc[at, c, 24:48] = sides
    early_copies = [
        remote(agsrc.at[x, ((z + d) % 8) // 4], early.at[h, z], ag_s.at[0], ag_r.at[0], z_peer(d))
        for d in FAR_Z
    ]
    start_all(early_copies)
    early[h, z] = agsrc[x, block]
    minus = [eye_less(mm(w1[at][0:64], w1[at + 1][0:64])) for at in (0, 2)]
    inverse = invert([pick(minus[0], minus[1])], False)
    share(2)
    t1 = []
    for even in (0, 2):
        low, high = w1[even], w1[even + 1]
        one = mm(high[64:152] - mm(low[64:152], high[0:64]), inverse[even // 2])
        t1 += [one, low[64:152] - mm(one, low[0:64])]
        couple[even // 2, 0] = low[0:64]
        couple[even // 2, 1] = high[0:64]
        couple[even // 2, 2] = inverse[even // 2]
    for at in range(4):
        second_t[at] = t1[at][0:64]
    pass_on(u_direct, u_onward, 1)
    share_copies[2].wait_recv()

    w2 = [after_zero(2, at) for at in range(4)]
    p2 = [w2[at][64:152] - mm(t1[at], w2[at][0:64]) for at in range(4)]
    low, high = p2[0] + p2[1], p2[2] + p2[3]
    own = jnp.where(x < 2, low, high)
    sib = jnp.where(x < 2, high, low)
    late[h * 8 + z] = pick(own[64:88], sib[64:88])
    late_copies = [
        remote(late.at[h * 8 + z], late.at[h * 8 + z], ag_s.at[1], ag_r.at[1], core_peer(d)) for d in FAR_CORE
    ]
    hear(3)
    start_all(late_copies)
    pass_on(u_direct, u_onward, 2)
    inverse = invert([eye_less(mm(own[0:64], sib[0:64]))], False)[0]
    wait_all(early.at[h, 0:7], ag_r.at[0])
    early_share = remote(early.at[h], early.at[h], ad_s.at[0], ad_r.at[0], partner)
    go(early_share)

    a_01 = first_t[x, block, 0:64]
    a_02 = first_t[x, block, 64:128]
    a_12 = second_t[x]
    c_1 = mm(inverse, a_12)
    c_0 = mm(inverse, a_02) - mm(c_1, a_01)
    last_01 = -pick(c_0, c_1)
    last_2 = inverse[:, :64]
    last_high, last_low = split(jnp.concatenate([last_01, last_2], axis=1))
    for l in range(LEVELS):
        for copy in u_onward[l]:
            copy.wait_recv()
    place = lax.broadcasted_iota(jnp.int32, (64, 1), 0)
    kept = jnp.concatenate([jnp.where(place < ranks_ref[l], 1.0, 0.0) for l in range(LEVELS)], axis=0)
    for part in range(4):
        span = slice(512 * part, 512 * part + 512)
        panel_high, panel_low = split(uall_ref[:, :, :, :, span].reshape(192, 512) * kept)
        last = dot(last_high, panel_high) + (dot(last_low, panel_high) + dot(last_high, panel_low))
        last_h, last_l = split(last * weight[:, span])
        right_ref[0:64, span] = last_h
        right_ref[64:128, span] = last_h
        right_ref[128:192, span] = last_l
        front_ref[0:128, span] = panel_high[0:128]
        front_ref[128:256, span] = panel_low[0:128]

    early_share.wait_recv()
    t_0 = early[:, :, 0:24].reshape(COLS, 128)
    q_even, q_odd = both(early[:, :, 24:48].reshape(COLS, 128))
    t_even = mm(q_odd - mm(q_even, couple[x // 2, 1]), couple[x // 2, 2])
    t_odd = q_even - mm(t_even, couple[x // 2, 0])
    t_1 = jnp.where(x % 2 == 0, t_even, t_odd)
    t_0 = t_0 - mm(t_1, a_01)
    front_high, front_low = split(pick(t_0, t_1))
    front_left = jnp.concatenate([front_high, front_low], axis=1)
    for part in range(4):
        span = slice(512 * part, 512 * part + 512)
        panel_high = front_ref[0:128, span]
        front = dot(front_left, jnp.concatenate([panel_high, panel_high], axis=0)) + dot(
            front_high, front_ref[128:256, span]
        )
        sum_ref[:, span] = lhs[0:COLS, span].astype(jnp.float32) * over[:, span] - front * weight[:, span]

    for copy in sent:
        copy.wait_send()
    for l in range(LEVELS):
        wait_all(chip.at[l, 0:7], z_s.at[l])
        wait_all(ubuf.at[l, h, 0:15], h_s.at[l])
        wait_all(bbuf.at[l, 0:3], b_s.at[l])
    wait_all(early.at[h, 0:7], ag_s.at[0])
    wait_all(late.at[0:15], ag_r.at[1])
    q_own, q_sib = both(late[...].reshape(COLS, 128))
    rest = q_sib - mm(q_own, sib[0:64])
    rest_high = rest.astype(jnp.bfloat16).astype(jnp.float32)
    left_ref[:, 0:128] = pick(rest_high, rest - rest_high).astype(jnp.bfloat16)
    left_ref[:, 128:192] = rest_high.astype(jnp.bfloat16)[:, :64]

    wait_all(late.at[0:15], ag_s.at[1])


def final_kernel(width, sum_ref, left_ref, right_ref, out_ref):
    span = pl.ds(pl.multiple_of(pl.program_id(0) * width, width), width)
    out_ref[...] = sum_ref[:, span] - dot(left_ref[...], right_ref[:, span])


def local(basis_u, basis_v, leaf_diag, right_side, leaf_len, ranks):
    f32 = jnp.float32
    diag = leaf_diag.reshape(1, ROWS)
    vmem = pl.BlockSpec(memory_space=pltpu.VMEM)
    dma = pltpu.SemaphoreType.DMA
    total, left, right = pl.pallas_call(
        solve_kernel,
        name="gather_and_solve",
        out_shape=(
            pltpu.VMEM((COLS, ROWS), f32),
            pltpu.VMEM((COLS, 192), jnp.bfloat16),
            pltpu.VMEM((192, ROWS), jnp.bfloat16),
        ),
        in_specs=[pl.BlockSpec(memory_space=pltpu.SMEM)] + [pl.BlockSpec(memory_space=pltpu.HBM)] * 5,
        out_specs=(vmem, vmem, vmem),
        scratch_shapes=[
            pltpu.SMEM((LEVELS,), jnp.int32),
            pltpu.VMEM((1, ROWS), f32),
            pltpu.VMEM((LEVELS, 4, 2, 8, ROWS), f32),
            pltpu.VMEM((LEVELS, 4, 2, 8, ROWS), f32),
            pltpu.VMEM((COLS + 96, ROWS), jnp.bfloat16),
            pltpu.VMEM((LEVELS, 2, 8, 24, 128), f32),
            pltpu.VMEM((LEVELS, 8, 24, 128), f32),
            pltpu.VMEM((LEVELS, 8, 24, 128), f32),
            pltpu.VMEM((LEVELS, 8, 24, 128), f32),
            pltpu.VMEM((LEVELS, 2, 16, 24, 128), f32),
            pltpu.VMEM((LEVELS, 4, 24, 128), f32),
            pltpu.VMEM((4, 2, 48, 128), f32),
            pltpu.VMEM((2, 3, 64, 128), f32),
            pltpu.VMEM((4, 2, 128, 128), f32),
            pltpu.VMEM((4, 64, 128), f32),
            pltpu.VMEM((2, 8, 48, 128), f32),
            pltpu.VMEM((16, 24, 128), f32),
            pltpu.VMEM((256, ROWS), jnp.bfloat16),
            pltpu.SemaphoreType.REGULAR((4,)),
            dma((5,)),
            dma((LEVELS, 4)), dma((LEVELS, 4)),
            dma((LEVELS, 4)), dma((LEVELS, 4)),
            dma((LEVELS,)), dma((LEVELS,)),
            dma((LEVELS,)), dma((LEVELS,)),
            dma((LEVELS,)), dma((LEVELS,)),
            dma((LEVELS,)), dma((LEVELS,)),
            dma((LEVELS,)), dma((LEVELS,)),
            dma((2,)), dma((2,)),
            dma((1,)), dma((1,)),
        ],
        compiler_params=pltpu.CompilerParams(
            collective_id=0, has_side_effects=True, vmem_limit_bytes=40 * 1024 * 1024
        ),
    )(
        leaf_len,
        *[
            pltpu.with_memory_space_constraint(array, pltpu.HBM)
            for array in (
                ranks,
                diag,
                basis_v.reshape(LEVELS, 2, 8, ROWS),
                basis_u.reshape(LEVELS, 2, 8, ROWS),
                right_side,
            )
        ]
    )
    width = 1024
    return pl.pallas_call(
        functools.partial(final_kernel, width),
        name="add_last_panel",
        grid=(ROWS // width,),
        out_shape=jax.ShapeDtypeStruct((COLS, ROWS), f32),
        in_specs=[vmem, vmem, vmem],
        out_specs=pl.BlockSpec((COLS, width), lambda i: (0, i)),
        compiler_params=pltpu.CompilerParams(vmem_limit_bytes=32 * 1024 * 1024),
        cost_estimate=pl.CostEstimate(flops=2 * COLS * 192 * ROWS, bytes_accessed=7200000, transcendentals=0),
    )(total, left, right)


def solution(mesh):
    in_specs = (
        P(None, "col", ("node", "row")),
        P(None, "col", ("node", "row")),
        P(("node", "row")),
        P("col", ("node", "row")),
        P(("node", "row")),
        P(),
    )
    out_specs = P("col", ("node", "row"))
    return jax.shard_map(local, mesh=mesh, in_specs=in_specs, out_specs=out_specs, check_vma=False)
```
